1024 devices in a mesh: dom: 64 (over x, y), within: 16 (over z, core).
Axes of the slice: x: 8, y: 8, z: 8, core: 2. Of those that a mesh axis runs over, the one named last changes fastest.
Arguments:
- right_side: float32 [64, 4, 32, 64, 128], P('dom', None, 'within'), may hold values from -6 to 6
- initial: float32 [64, 4, 32, 64, 128], P('dom', None, 'within'), may hold values from -6 to 6
- block_inverse: float32 [64, 4, 4, 32, 64, 128], P('dom', None, None, 'within')
- conductivity: float32 [64, 32, 64, 128], P('dom', 'within'), may hold values from 0.5 to 2
- stencil: float32 [64, 6, 4, 4], P('dom'), may hold values from -1.5 to 1.5
- coupling_source: int32 [64, 16, 64], P('dom', 'within'), may hold values from 0 to 63, as said below
- coupling_target: int32 [64, 16, 64], P('dom', 'within'), may hold values from 0 to 3
- coupling_weight: float32 [64, 16, 64, 4, 4], P('dom', 'within'), may hold values from -3 to 3
- live_count: int32 [64, 16], P('dom', 'within'), may hold values from 1 to 64, as said below
- send_faces: int32 [64, 16, 64, 2], P('dom', 'within'), may hold values from 0 to 3, as said below
Outputs:
- smoothed: float32 [64, 4, 32, 64, 128], P('dom', None, 'within')
The draws below stay inside these ranges and needn't reach their ends.
Inputs may be any that keep to these rules, and one draw needn't show every extreme that they name: `coupling_source`: entry e of group g at slab w comes from group (g + h + e // 2) mod 64, where 1 <= h <= 32 is fixed for each group and slab. `live_count`: for each group and slab the entries at or beyond the count are ignored; in every slab some group has all 64 entries live. `send_faces`: slots that no entry reads hold 0.
All inputs are finite; a program needn't handle non-finite values.
Results may differ from the reference program's by a relative error of at most 0.0001.
Values sent between devices are 32-bit elements; how exact they have to be, the bound alone decides.
No kernel may reach another device: no remote copies, remote signals or barrier semaphores. Data moves between devices by JAX's collectives and lax.ppermute only.
A program may use at most 32 MiB of HBM per device.

```python
import math
import jax
import jax.numpy as jnp
from jax import lax

V = 4
PART_DEV = 1
CX = 2
PY = 64
PZ = 128
SWEEPS = 3
SLOT = 2
GROUPS = 64
SLABS = 16
HOPS = 32
REC = 64
FACES = 4
PARTS_SIZE = 64
NX = 32


def route_plan(key):
    shift = jax.random.randint(jax.random.fold_in(key, 101), (GROUPS, SLABS, 1), 1, GROUPS - HOPS + 1)
    entry_ids = jnp.arange(REC, dtype=jnp.int32)[None, None, :]
    group_ids = jnp.arange(GROUPS, dtype=jnp.int32)[:, None, None]
    slab_ids = jnp.zeros((GROUPS, SLABS, REC), jnp.int32) + jnp.arange(SLABS, dtype=jnp.int32)[None, :, None]
    source = (group_ids + shift + entry_ids // SLOT) % GROUPS
    faces = jax.random.randint(jax.random.fold_in(key, 102), (GROUPS, SLABS, REC), 0, FACES)
    dest = jnp.zeros((GROUPS, SLABS, REC), jnp.int32) + group_ids
    slot_ids = jnp.zeros((GROUPS, SLABS, REC), jnp.int32) + entry_ids % SLOT
    table = jnp.zeros((GROUPS, SLABS, GROUPS, SLOT), jnp.int32).at[source, slab_ids, dest, slot_ids].set(faces)
    return (source.astype(jnp.int32), table)


def draw_coupling_source(key, part):
    return route_plan(key)[0]


def draw_send_faces(key, part):
    return route_plan(key)[1]


def draw_live_count(key, part):
    key = jax.random.fold_in(key, 7)
    first = jax.random.randint(jax.random.fold_in(key, 1), (GROUPS, SLABS), 0, REC)
    second = jax.random.randint(jax.random.fold_in(key, 2), (GROUPS, SLABS), 0, REC)
    counts = REC - first * second // max(REC - 1, 1)
    chosen = jax.random.randint(jax.random.fold_in(key, 3), (1, SLABS), 0, GROUPS)
    group_ids = jnp.arange(GROUPS, dtype=jnp.int32)[:, None]
    return jnp.clip(jnp.where(group_ids == chosen, REC, counts), 1, REC).astype(jnp.int32)


def draw_block_inverse(key, part):
    key = jax.random.fold_in(key, 11)
    shape = (PARTS_SIZE, V, V, NX, PY, PZ)
    eye = (jnp.arange(V)[:, None] == jnp.arange(V)[None, :])[None, :, :, None, None, None]
    diagonal = jax.random.uniform(jax.random.fold_in(key, 1), shape, jnp.float32, 0.1, 0.25)
    offdiag = jnp.clip(0.04 * jax.random.normal(jax.random.fold_in(key, 2), shape, jnp.float32), -0.12, 0.12)
    return jnp.where(eye, diagonal, offdiag).astype(jnp.float32)


def place_ends(values, rng, low, high):
    extent = values.shape
    place = [jax.random.randint(jax.random.fold_in(rng, axis), (), 0, extent[axis]) for axis in range(len(extent))]
    values = values.at[tuple(place)].set(low)
    longest = extent.index(max(extent))
    place[longest] = (place[longest] + 1) % extent[longest]
    return values.at[tuple(place)].set(high)


def shard_levels(stream_key, shape, shards, low, largest):
    gain = 1.0
    for axis_at, parts in shards:
        steps = jax.random.uniform(jax.random.fold_in(jax.random.fold_in(stream_key, 6), axis_at), (parts,), jnp.float32, low / len(shards), largest / len(shards))
        gain = gain * jnp.repeat(jnp.exp(steps), shape[axis_at] // parts).reshape((-1,) + (1,) * (len(shape) - 1 - axis_at))
    return gain


def normal_values(stream_key, dims, deviation, most, pieces=(), kind=jnp.bfloat16):
    entries = deviation * jax.random.normal(stream_key, dims, jnp.float32)
    if pieces:
        entries = entries * shard_levels(stream_key, dims, pieces, -0.22, 0.18)
    return jnp.clip(entries, -most, most).astype(kind)


def setup_inputs(seed: int = 0) -> dict:
    keys = jax.random.split(jax.random.key(seed), 11)
    return {
        "right_side": normal_values(keys[0], (PARTS_SIZE, V, NX, PY, PZ), 1.0, 6.0, ((0, 64), (2, 16)), jnp.float32),
        "initial": normal_values(keys[1], (PARTS_SIZE, V, NX, PY, PZ), 1.0, 6.0, ((0, 64), (2, 16)), jnp.float32),
        "block_inverse": draw_block_inverse(jax.random.fold_in(keys[10], 71), 0),
        "conductivity": jnp.clip(jnp.exp(math.log(2.0) - 1.3862944 * jax.random.uniform(keys[3], (PARTS_SIZE, NX, PY, PZ), jnp.float32) ** shard_levels(keys[3], (PARTS_SIZE, NX, PY, PZ), ((0, 64), (1, 16)), -0.2, 0.2)), 0.5, 2.0),
        "stencil": normal_values(keys[4], (PARTS_SIZE, 6, V, V), 16 ** -0.5, 1.5, ((0, 64),), jnp.float32),
        "coupling_source": draw_coupling_source(jax.random.fold_in(keys[10], 71), 0),
        "coupling_target": place_ends(jax.random.randint(keys[6], (GROUPS, SLABS, REC), 0, FACES), jax.random.fold_in(keys[6], 1), 0, FACES - 1).astype(jnp.int32),
        "coupling_weight": normal_values(keys[7], (GROUPS, SLABS, REC, V, V), V ** -0.5, 3.0, ((0, 64), (1, 16)), jnp.float32),
        "live_count": draw_live_count(jax.random.fold_in(keys[10], 71), 0),
        "send_faces": draw_send_faces(jax.random.fold_in(keys[10], 71), 0),
    }


relax_weight = 0.8


def apply_block(matrix, values):
    total = jnp.zeros(values.shape, jnp.float32)
    for column in range(values.shape[1]):
        total = total + matrix[:, :, column][:, :, None, None, None] * values[:, column][:, None]
    return total


def neighbour_sum(padded, stencil):
    shifted = [padded[:, :, :-2, 1:-1, 1:-1], padded[:, :, 2:, 1:-1, 1:-1],
               padded[:, :, 1:-1, :-2, 1:-1], padded[:, :, 1:-1, 2:, 1:-1],
               padded[:, :, 1:-1, 1:-1, :-2], padded[:, :, 1:-1, 1:-1, 2:]]
    total = apply_block(stencil[:, 0], shifted[0])
    for direction in range(1, 6):
        total = total + apply_block(stencil[:, direction], shifted[direction])
    return total


def reference(right_side, initial, block_inverse, conductivity, stencil, coupling_source, coupling_target, coupling_weight, live_count, send_faces):
    group_ids = jnp.arange(GROUPS, dtype=jnp.int32)[:, None, None]
    slab_ids = jnp.arange(SLABS, dtype=jnp.int32)[None, :, None]
    entry_ids = jnp.arange(REC, dtype=jnp.int32)[None, None, :]
    source_face = send_faces[coupling_source, slab_ids, group_ids, entry_ids % SLOT]
    source_part = coupling_source * PART_DEV + source_face // (2 * CX)
    source_x = slab_ids * CX + (source_face // 2) % CX
    source_y = (source_face % 2) * (PY - 1)
    target_part = group_ids * PART_DEV + coupling_target // (2 * CX)
    target_x = slab_ids * CX + (coupling_target // 2) % CX
    target_y = (coupling_target % 2) * (PY - 1)
    live = (entry_ids < live_count[:, :, None]).astype(jnp.float32)
    weights = coupling_weight * live[:, :, :, None, None]
    field = initial
    for sweep_index in range(SWEEPS):
        padded = jnp.pad(field, ((0, 0), (0, 0), (1, 1), (1, 1), (1, 1)))
        load = right_side + conductivity[:, None] * neighbour_sum(padded, stencil)
        strips = field[source_part, :, source_x, source_y, :]
        added = jnp.einsum("gsrab,gsrbz->gsraz", weights, strips, precision=lax.Precision.HIGHEST)
        load = load.at[target_part, :, target_x, target_y, :].add(added)
        field = (1.0 - relax_weight) * field + relax_weight * apply_block6(block_inverse, load)
    return field


def apply_block6(matrix, values):
    total = jnp.zeros(values.shape, jnp.float32)
    for column in range(values.shape[1]):
        total = total + matrix[:, :, column] * values[:, column][:, None]
    return total
```

```python
import functools

import jax
import jax.numpy as jnp
from jax import lax
from jax.experimental import pallas as pl
from jax.experimental.pallas import tpu as pltpu
from jax.sharding import PartitionSpec as P

SWEEPS = 3
V = 4
CX = 2
FACES = 4
SLOT = 2

relax_weight = 0.8

VMEM = pl.BlockSpec(memory_space=pltpu.VMEM)
SMEM = pl.BlockSpec(memory_space=pltpu.SMEM)
PARAMS = pltpu.CompilerParams(vmem_limit_bytes=24 * 1024 * 1024)


def face_place(face, rows):
    return face // 2, (rows - 1) * (face % 2)


def fill_send(faces_ref, strips_ref, send_ref):
    for group in range(send_ref.shape[0]):
        for slot in range(SLOT):
            face = faces_ref[group * SLOT + slot]
            send_ref[group, slot * V : (slot + 1) * V, :] = strips_ref[face]


def first_kernel(faces_ref, field_ref, send_ref, strips):
    rows = field_ref.shape[2]
    for face in range(FACES):
        plane, row = face_place(face, rows)
        for var in range(V):
            strips[face, var : var + 1, :] = field_ref[var, plane, row : row + 1, :]
    fill_send(faces_ref, strips, send_ref)


def first_send(faces, field):
    groups = faces.shape[0] // SLOT
    z = field.shape[-1]
    return pl.pallas_call(
        first_kernel,
        out_shape=jax.ShapeDtypeStruct((groups, SLOT * V, z), jnp.float32),
        in_specs=[SMEM, VMEM],
        out_specs=VMEM,
        scratch_shapes=[pltpu.VMEM((FACES, V, z), jnp.float32)],
        compiler_params=PARAMS,
        cost_estimate=pl.CostEstimate(flops=0, bytes_accessed=512 * 1024, transcendentals=0),
    )(faces, field)


def local_kernel(
    first,
    stencil_ref,
    plane0_ref,
    plane1_ref,
    low_ref,
    high_ref,
    right_ref,
    conductivity_ref,
    inverse_ref,
    next0_ref,
    next1_ref,
    strips_ref,
    *maybe_edge,
):
    rows, lanes = plane0_ref.shape[1:]
    row_ids = lax.broadcasted_iota(jnp.int32, (rows, lanes), 0)
    lane_ids = lax.broadcasted_iota(jnp.int32, (rows, lanes), 1)
    around = (low_ref, plane0_ref, plane1_ref, high_ref)
    outs = (next0_ref, next1_ref)
    for plane in range(CX):
        below, here, above = around[plane : plane + 3]
        sums = [jnp.zeros((rows, lanes), jnp.float32) for _ in range(V)]
        for col in range(V):
            value = here[col]
            shifted = (
                below[col],
                above[col],
                jnp.where(row_ids == 0, 0.0, pltpu.roll(value, 1, 0)),
                jnp.where(row_ids == rows - 1, 0.0, pltpu.roll(value, rows - 1, 0)),
                jnp.where(lane_ids == 0, 0.0, pltpu.roll(value, 1, 1)),
                jnp.where(lane_ids == lanes - 1, 0.0, pltpu.roll(value, lanes - 1, 1)),
            )
            for direction in range(6):
                for var in range(V):
                    coef = stencil_ref[(direction * V + var) * V + col]
                    sums[var] = sums[var] + coef * shifted[direction]
        cond = conductivity_ref[plane]
        loads = [right_ref[var, plane] + cond * sums[var] for var in range(V)]
        for var in range(V):
            total = inverse_ref[var, 0, plane] * loads[0]
            for col in range(1, V):
                total = total + inverse_ref[var, col, plane] * loads[col]
            outs[plane][var] = (1.0 - relax_weight) * here[var] + relax_weight * total
    for face in range(FACES):
        plane, row = face_place(face, rows)
        for var in range(V):
            at = face * V + var
            strips_ref[at : at + 1, :] = outs[plane][var, row : row + 1, :]
            if first:
                for col in range(V):
                    maybe_edge[0][col, at : at + 1, :] = (
                        relax_weight * inverse_ref[var, col, plane, row : row + 1, :]
                    )


def local_part(first, stencil, plane0, plane1, low, high, right, conductivity, inverse):
    shape = jax.ShapeDtypeStruct(plane0.shape, jnp.float32)
    z = plane0.shape[-1]
    out_shape = [shape, shape, jax.ShapeDtypeStruct((FACES * V, z), jnp.float32)]
    if first:
        out_shape.append(jax.ShapeDtypeStruct((V, FACES * V, z), jnp.float32))
    return pl.pallas_call(
        functools.partial(local_kernel, first),
        out_shape=out_shape,
        in_specs=[SMEM] + [VMEM] * 7,
        out_specs=[VMEM] * len(out_shape),
        compiler_params=PARAMS,
        cost_estimate=pl.CostEstimate(
            flops=4_000_000, bytes_accessed=2 * 1024 * 1024, transcendentals=0
        ),
    )(stencil, plane0, plane1, low, high, right, conductivity, inverse)


def new_strips(start_ref, matrix_ref, edge_ref, strips_ref, got_ref):
    groups = got_ref.shape[0]
    hops = matrix_ref.shape[1] // (SLOT * V)
    start = start_ref[0]
    values = jnp.concatenate(
        [got_ref[lax.rem(start + hop, groups)] for hop in range(hops)], axis=0
    )
    added = jnp.dot(
        matrix_ref[...],
        values,
        precision=lax.Precision.HIGHEST,
        preferred_element_type=jnp.float32,
    )
    total = strips_ref[...]
    count = FACES * V
    for col in range(V):
        total = total + edge_ref[col] * added[col * count : (col + 1) * count]
    return total


def strip_kernel(
    start_ref, faces_ref, matrix_ref, edge_ref, strips_ref, got_ref, send_ref, new_ref, scratch
):
    total = new_strips(start_ref, matrix_ref, edge_ref, strips_ref, got_ref)
    new_ref[...] = total
    for face in range(FACES):
        scratch[face] = total[face * V : (face + 1) * V]
    fill_send(faces_ref, scratch, send_ref)


def strip_part(start, faces, matrix, edge, strips, got):
    return pl.pallas_call(
        strip_kernel,
        out_shape=[
            jax.ShapeDtypeStruct(got.shape, jnp.float32),
            jax.ShapeDtypeStruct(strips.shape, jnp.float32),
        ],
        in_specs=[SMEM, SMEM, VMEM, VMEM, VMEM, VMEM],
        out_specs=[VMEM, VMEM],
        scratch_shapes=[pltpu.VMEM((FACES, V, strips.shape[-1]), jnp.float32)],
        compiler_params=PARAMS,
        cost_estimate=pl.CostEstimate(flops=0, bytes_accessed=512 * 1024, transcendentals=0),
    )(start, faces, matrix, edge, strips, got)


def patch_kernel(new_ref, old0_ref, old1_ref, plane0_ref, plane1_ref):
    rows = plane0_ref.shape[1]
    plane0_ref[...] = old0_ref[...]
    plane1_ref[...] = old1_ref[...]
    outs = (plane0_ref, plane1_ref)
    for face in range(FACES):
        plane, row = face_place(face, rows)
        for var in range(V):
            at = face * V + var
            outs[plane][var, row : row + 1, :] = new_ref[at : at + 1, :]


def patch_part(new, plane0, plane1):
    shape = jax.ShapeDtypeStruct(plane0.shape, jnp.float32)
    return pl.pallas_call(
        patch_kernel,
        out_shape=[shape, shape],
        in_specs=[VMEM] * 3,
        out_specs=[VMEM] * 2,
        compiler_params=PARAMS,
        cost_estimate=pl.CostEstimate(flops=0, bytes_accessed=512 * 1024, transcendentals=0),
    )(new, plane0, plane1)


def last_kernel(
    start_ref, matrix_ref, edge_ref, strips_ref, got_ref, plane0_ref, plane1_ref, out_ref
):
    rows = plane0_ref.shape[1]
    for var in range(V):
        out_ref[var, 0] = plane0_ref[var]
        out_ref[var, 1] = plane1_ref[var]
    total = new_strips(start_ref, matrix_ref, edge_ref, strips_ref, got_ref)
    for face in range(FACES):
        plane, row = face_place(face, rows)
        for var in range(V):
            at = face * V + var
            out_ref[var, plane, row : row + 1, :] = total[at : at + 1]


def last_part(start, matrix, edge, strips, got, plane0, plane1):
    return pl.pallas_call(
        last_kernel,
        out_shape=jax.ShapeDtypeStruct((V, CX) + plane0.shape[1:], jnp.float32),
        in_specs=[SMEM] + [VMEM] * 6,
        out_specs=VMEM,
        compiler_params=PARAMS,
        cost_estimate=pl.CostEstimate(flops=0, bytes_accessed=512 * 1024, transcendentals=0),
    )(start, matrix, edge, strips, got, plane0, plane1)


def per_device(
    right_side,
    initial,
    block_inverse,
    conductivity,
    stencil,
    coupling_source,
    coupling_target,
    coupling_weight,
    live_count,
    send_faces,
):
    field = initial[0]
    right = right_side[0]
    inverse = block_inverse[0]
    cond = conductivity[0]
    coefs = stencil[0].reshape(-1)
    start = coupling_source[0, 0, 0:1]
    targets = coupling_target[0, 0]
    weights = coupling_weight[0, 0]
    faces = send_faces[0, 0].reshape(-1)
    entries = targets.shape[0]

    send = first_send(faces, field)

    live = jnp.arange(entries, dtype=jnp.int32) < live_count[0, 0]
    face_ids = jnp.arange(FACES, dtype=jnp.int32)
    chosen = (targets[None, :] == face_ids[:, None]) & live[None, :]
    by_col = jnp.transpose(weights, (1, 0, 2))
    matrix = jnp.where(chosen[None, :, None, :, None], by_col[:, None, None], 0.0)
    matrix = jnp.broadcast_to(matrix, (V, FACES, V, entries, V))
    matrix = matrix.reshape(V * FACES * V, entries * V)

    count = lax.axis_size("within")
    forward = [(i, i + 1) for i in range(count - 1)]
    backward = [(i + 1, i) for i in range(count - 1)]

    plane0, plane1 = field[:, 0], field[:, 1]
    edge = None
    for sweep in range(SWEEPS):
        got = lax.all_to_all(send, "dom", 0, 0, tiled=True)
        high = lax.ppermute(plane0, "within", backward)
        low = lax.ppermute(plane1, "within", forward)
        results = local_part(
            sweep == 0, coefs, plane0, plane1, low, high, right, cond, inverse
        )
        next0, next1, strips = results[:3]
        if sweep == 0:
            edge = results[3]
        if sweep < SWEEPS - 1:
            send, new = strip_part(start, faces, matrix, edge, strips, got)
            plane0, plane1 = patch_part(new, next0, next1)
        else:
            out = last_part(start, matrix, edge, strips, got, next0, next1)
    return out[None]


def solution(mesh):
    in_specs = (
        P("dom", None, "within", None, None),
        P("dom", None, "within", None, None),
        P("dom", None, None, "within", None, None),
        P("dom", "within", None, None),
        P("dom", None, None, None),
        P("dom", "within", None),
        P("dom", "within", None),
        P("dom", "within", None, None, None),
        P("dom", "within"),
        P("dom", "within", None, None),
    )
    out_specs = P("dom", None, "within", None, None)
    return jax.shard_map(
        per_device, mesh=mesh, in_specs=in_specs, out_specs=out_specs, check_vma=False
    )
```

```python
import functools

import jax
import jax.numpy as jnp
from jax import lax
from jax.experimental import pallas as pl
from jax.experimental.pallas import tpu as pltpu
from jax.sharding import PartitionSpec as P

SWEEPS = 3
V = 4
CX = 2
FACES = 4
SLOT = 2
ROWS = FACES * V

relax_weight = 0.8

VMEM = pl.BlockSpec(memory_space=pltpu.VMEM)
SMEM = pl.BlockSpec(memory_space=pltpu.SMEM)
PARAMS = pltpu.CompilerParams(vmem_limit_bytes=24 * 1024 * 1024)


def call(kernel, out_shape, in_specs, args, scratch=(), flops=0, moved=512 * 1024):
    single = not isinstance(out_shape, list)
    return pl.pallas_call(
        kernel,
        out_shape=out_shape,
        in_specs=in_specs,
        out_specs=VMEM if single else [VMEM] * len(out_shape),
        scratch_shapes=list(scratch),
        compiler_params=PARAMS,
        cost_estimate=pl.CostEstimate(flops=flops, bytes_accessed=moved, transcendentals=0),
    )(*args)


def f32(*shape):
    return jax.ShapeDtypeStruct(shape, jnp.float32)


def inner_plane():
    return 1 - lax.rem(lax.axis_index("within"), 2)


def edge_rows(rows):
    return (0, rows - 1)


def first_kernel(faces_ref, field_ref, send_ref, strips_ref, scratch):
    rows = field_ref.shape[2]
    for plane in range(CX):
        for side, row in enumerate(edge_rows(rows)):
            for var in range(V):
                value = field_ref[var, plane, row : row + 1, :]
                scratch[plane * 2 + side, var : var + 1, :] = value
                at = side * V + var
                strips_ref[plane, at : at + 1, :] = value
    for group in range(send_ref.shape[0]):
        for slot in range(SLOT):
            send_ref[group, slot * V : (slot + 1) * V, :] = scratch[faces_ref[slot, group]]


def first_part(faces, field):
    groups, z = faces.shape[1], field.shape[-1]
    return call(
        first_kernel,
        [f32(groups, SLOT * V, z), f32(CX, 2 * V, z)],
        [SMEM, VMEM],
        (faces, field),
        scratch=[pltpu.VMEM((FACES, V, z), jnp.float32)],
    )


def split_kernel(strips_ref, field_ref, inner_ref, outer_ref):
    rows = inner_ref.shape[1]
    at = inner_plane()
    for ref, plane in ((inner_ref, at), (outer_ref, 1 - at)):
        for var in range(V):
            ref[var] = field_ref[var, plane]
        for side, row in enumerate(edge_rows(rows)):
            for var in range(V):
                here = side * V + var
                ref[var, row : row + 1, :] = strips_ref[plane, here : here + 1, :]


def split_part(strips, field):
    shape = f32(V, field.shape[2], field.shape[3])
    return call(split_kernel, [shape, shape], [VMEM] * 2, (strips, field))


def patch_kernel(strips_ref, old_inner_ref, old_outer_ref, inner_ref, outer_ref):
    rows = inner_ref.shape[1]
    at = inner_plane()
    for ref, old, plane in (
        (inner_ref, old_inner_ref, at),
        (outer_ref, old_outer_ref, 1 - at),
    ):
        ref[...] = old[...]
        for side, row in enumerate(edge_rows(rows)):
            for var in range(V):
                here = side * V + var
                ref[var, row : row + 1, :] = strips_ref[plane, here : here + 1, :]


def patch_part(strips, inner, outer):
    shape = f32(*inner.shape)
    return call(patch_kernel, [shape, shape], [VMEM] * 3, (strips, inner, outer))


def setup_kernel(
    source_ref, live_ref, faces_ref, target_ref, weight_ref, matrix_ref, mask_ref
):
    entries = target_ref.shape[1]
    groups = mask_ref.shape[0]
    columns = matrix_ref.shape[1]
    row_ids = lax.broadcasted_iota(jnp.int32, (ROWS, entries), 0)
    entry_ids = lax.broadcasted_iota(jnp.int32, (ROWS, entries), 1)
    chosen = (row_ids // V == target_ref[...]) & (entry_ids < live_ref[0, 0])
    place = lax.broadcasted_iota(jnp.int32, (entries, columns), 0) + SLOT * source_ref[0, 0]
    place = jnp.where(place >= SLOT * groups, place - SLOT * groups, place)
    column_ids = lax.broadcasted_iota(jnp.int32, (entries, columns), 1)
    matrix = jnp.zeros((V * ROWS, columns), jnp.float32)
    for col in range(V):
        spread = jnp.concatenate(
            [jnp.where(chosen, weight_ref[var, col : col + 1, :], 0.0) for var in range(V)],
            axis=0,
        )
        order = (column_ids == place * V + col).astype(jnp.float32)
        matrix = matrix + jnp.dot(
            spread,
            order,
            precision=lax.Precision.HIGHEST,
            preferred_element_type=jnp.float32,
        )
    high = matrix.astype(jnp.bfloat16)
    matrix_ref[: V * ROWS, :] = high
    matrix_ref[V * ROWS :, :] = (matrix - high.astype(jnp.float32)).astype(jnp.bfloat16)
    tile_rows = lax.broadcasted_iota(jnp.int32, mask_ref.shape[1:], 0)
    for group in range(groups):
        mask_ref[group] = jnp.where(tile_rows < V, faces_ref[0, group], faces_ref[1, group])


def setup_part(source, live, faces, target, weight, z):
    groups = faces.shape[1]
    return call(
        setup_kernel,
        [
            jax.ShapeDtypeStruct((2 * V * ROWS, groups * SLOT * V), jnp.bfloat16),
            jax.ShapeDtypeStruct((groups, SLOT * V, z), jnp.int32),
        ],
        [SMEM, SMEM, SMEM, VMEM, VMEM],
        (source, live, faces, target, weight),
    )


def local_kernel(
    first,
    stencil_ref,
    inner_ref,
    outer_ref,
    from_core_ref,
    from_chip_ref,
    right_ref,
    conductivity_ref,
    inverse_ref,
    next_inner_ref,
    next_outer_ref,
    strips_ref,
    *maybe_edge,
):
    rows, lanes = inner_ref.shape[1:]
    row_ids = lax.broadcasted_iota(jnp.int32, (rows, lanes), 0)
    lane_ids = lax.broadcasted_iota(jnp.int32, (rows, lanes), 1)
    at = inner_plane()
    for here, beside, outside, plane, out_ref in (
        (inner_ref, outer_ref, from_core_ref, at, next_inner_ref),
        (outer_ref, inner_ref, from_chip_ref, 1 - at, next_outer_ref),
    ):
        directions = (plane, 1 - plane, 2, 3, 4, 5)
        sums = [jnp.zeros((rows, lanes), jnp.float32) for _ in range(V)]
        for col in range(V):
            value = here[col]
            shifted = (
                outside[col],
                beside[col],
                jnp.where(row_ids == 0, 0.0, pltpu.roll(value, 1, 0)),
                jnp.where(row_ids == rows - 1, 0.0, pltpu.roll(value, rows - 1, 0)),
                jnp.where(lane_ids == 0, 0.0, pltpu.roll(value, 1, 1)),
                jnp.where(lane_ids == lanes - 1, 0.0, pltpu.roll(value, lanes - 1, 1)),
            )
            for direction, moved in zip(directions, shifted):
                for var in range(V):
                    sums[var] = sums[var] + stencil_ref[var, col, direction] * moved
        cond = conductivity_ref[plane]
        loads = [right_ref[var, plane] + cond * sums[var] for var in range(V)]
        for var in range(V):
            total = inverse_ref[var, 0, plane] * loads[0]
            for col in range(1, V):
                total = total + inverse_ref[var, col, plane] * loads[col]
            out_ref[var] = (1.0 - relax_weight) * here[var] + relax_weight * total
        for side, row in enumerate(edge_rows(rows)):
            for var in range(V):
                to = side * V + var
                strips_ref[plane, to : to + 1, :] = out_ref[var, row : row + 1, :]
                if first:
                    for col in range(V):
                        maybe_edge[0][col, plane, to : to + 1, :] = (
                            relax_weight * inverse_ref[var, col, plane, row : row + 1, :]
                        )


def local_part(first, stencil, inner, outer, from_core, from_chip, right, cond, inverse):
    z = inner.shape[-1]
    out_shape = [f32(*inner.shape), f32(*inner.shape), f32(CX, 2 * V, z)]
    if first:
        out_shape.append(f32(V, CX, 2 * V, z))
    return call(
        functools.partial(local_kernel, first),
        out_shape,
        [SMEM] + [VMEM] * 7,
        (stencil, inner, outer, from_core, from_chip, right, cond, inverse),
        flops=4_000_000,
        moved=2 * 1024 * 1024,
    )


def new_strips(matrix_ref, edge_ref, strips_ref, got_ref):
    groups, block, z = got_ref.shape
    values = got_ref[...].reshape(groups * block, z)
    high = values.astype(jnp.bfloat16)
    low = (values - high.astype(jnp.float32)).astype(jnp.bfloat16)
    count = V * ROWS
    both = jnp.dot(matrix_ref[...], high, preferred_element_type=jnp.float32)
    rest = jnp.dot(matrix_ref[:count, :], low, preferred_element_type=jnp.float32)
    added = both[:count] + (both[count:] + rest)
    tiles = []
    for plane in range(CX):
        total = strips_ref[plane]
        for col in range(V):
            begin = col * ROWS + plane * 2 * V
            total = total + edge_ref[col, plane] * added[begin : begin + 2 * V]
        tiles.append(total)
    return tiles


def strip_kernel(matrix_ref, edge_ref, strips_ref, got_ref, mask_ref, send_ref, new_ref):
    tiles = new_strips(matrix_ref, edge_ref, strips_ref, got_ref)
    upper = lax.broadcasted_iota(jnp.int32, tiles[0].shape, 0) < V
    faces = []
    for plane, tile in enumerate(tiles):
        new_ref[plane] = tile
        other = pltpu.roll(tile, V, 0)
        faces += [jnp.where(upper, tile, other), jnp.where(upper, other, tile)]
    for group in range(send_ref.shape[0]):
        mask = mask_ref[group]
        value = faces[FACES - 1]
        for face in range(FACES - 1):
            value = jnp.where(mask == face, faces[face], value)
        send_ref[group] = value


def strip_part(matrix, edge, strips, got, mask):
    return call(
        strip_kernel,
        [f32(*got.shape), f32(*strips.shape)],
        [VMEM] * 5,
        (matrix, edge, strips, got, mask),
    )


def last_kernel(matrix_ref, edge_ref, strips_ref, got_ref, inner_ref, outer_ref, out_ref):
    rows = inner_ref.shape[1]
    at = inner_plane()
    for ref, plane in ((inner_ref, at), (outer_ref, 1 - at)):
        for var in range(V):
            out_ref[var, plane] = ref[var]
    tiles = new_strips(matrix_ref, edge_ref, strips_ref, got_ref)
    for plane, tile in enumerate(tiles):
        for side, row in enumerate(edge_rows(rows)):
            for var in range(V):
                here = side * V + var
                out_ref[var, plane, row : row + 1, :] = tile[here : here + 1]


def last_part(matrix, edge, strips, got, inner, outer):
    return call(
        last_kernel,
        f32(V, CX, *inner.shape[1:]),
        [VMEM] * 6,
        (matrix, edge, strips, got, inner, outer),
    )


def per_device(
    right_side,
    initial,
    block_inverse,
    conductivity,
    stencil,
    coupling_source,
    coupling_target,
    coupling_weight,
    live_count,
    send_faces,
):
    field = initial[0]
    right = right_side[0]
    inverse = block_inverse[0]
    cond = conductivity[0]
    coefs = jnp.transpose(stencil[0], (1, 2, 0))
    weight = jnp.transpose(coupling_weight[0, 0], (1, 2, 0))
    faces = jnp.transpose(send_faces[0, 0], (1, 0))

    count = lax.axis_size("within")
    core_swap = [(i, i ^ 1) for i in range(count)]
    chip_swap = [(i, i + 1) for i in range(1, count - 1, 2)]
    chip_swap += [(j, i) for i, j in chip_swap]

    send, strips = first_part(faces, field)
    inner, outer = split_part(strips, field)
    matrix, mask = setup_part(
        coupling_source[0], live_count, faces, coupling_target[0], weight, field.shape[-1]
    )
    edge = None
    for sweep in range(SWEEPS):
        got = lax.all_to_all(send, "dom", 0, 0, tiled=True)
        from_chip = lax.ppermute(outer, "within", chip_swap)
        from_core = lax.ppermute(inner, "within", core_swap)
        results = local_part(
            sweep == 0, coefs, inner, outer, from_core, from_chip, right, cond, inverse
        )
        inner, outer, strips = results[:3]
        if sweep == 0:
            edge = results[3]
        if sweep < SWEEPS - 1:
            send, new = strip_part(matrix, edge, strips, got, mask)
            inner, outer = patch_part(new, inner, outer)
        else:
            out = last_part(matrix, edge, strips, got, inner, outer)
    return out[None]


def solution(mesh):
    in_specs = (
        P("dom", None, "within", None, None),
        P("dom", None, "within", None, None),
        P("dom", None, None, "within", None, None),
        P("dom", "within", None, None),
        P("dom", None, None, None),
        P("dom", "within", None),
        P("dom", "within", None),
        P("dom", "within", None, None, None),
        P("dom", "within"),
        P("dom", "within", None, None),
    )
    out_specs = P("dom", None, "within", None, None)
    return jax.shard_map(
        per_device, mesh=mesh, in_specs=in_specs, out_specs=out_specs, check_vma=False
    )
```

```python
import functools

import jax
import jax.numpy as jnp
from jax import lax
from jax.experimental import pallas as pl
from jax.experimental.pallas import tpu as pltpu
from jax.sharding import PartitionSpec as P

SWEEPS = 3
V = 4
CX = 2
FACES = 4
SLOT = 2
ROWS = FACES * V

relax_weight = 0.8

VMEM = pl.BlockSpec(memory_space=pltpu.VMEM)
SMEM = pl.BlockSpec(memory_space=pltpu.SMEM)
HBM = pl.BlockSpec(memory_space=pltpu.HBM)
PARAMS = pltpu.CompilerParams(vmem_limit_bytes=24 * 1024 * 1024)


def call(kernel, out_shape, in_specs, args, scratch=(), flops=0, moved=512 * 1024):
    single = not isinstance(out_shape, list)
    return pl.pallas_call(
        kernel,
        out_shape=out_shape,
        in_specs=in_specs,
        out_specs=VMEM if single else [VMEM] * len(out_shape),
        scratch_shapes=list(scratch),
        compiler_params=PARAMS,
        cost_estimate=pl.CostEstimate(flops=flops, bytes_accessed=moved, transcendentals=0),
    )(*args)


def in_hbm(*arrays):
    return tuple(pltpu.with_memory_space_constraint(array, pltpu.HBM) for array in arrays)


def f32(*shape):
    return jax.ShapeDtypeStruct(shape, jnp.float32)


def inner_plane():
    return 1 - lax.rem(lax.axis_index("within"), 2)


def edge_rows(rows):
    return (0, rows - 1)


def first_kernel(
    faces_hbm, field_hbm, send_ref, strips_ref, inner_ref, outer_ref, faces, edges, scratch, sems
):
    rows = field_hbm.shape[2]
    tile = edges.shape[3]
    at = inner_plane()
    copies = [
        pltpu.make_async_copy(faces_hbm, faces, sems.at[0]),
        pltpu.make_async_copy(field_hbm.at[:, :, pl.ds(0, tile)], edges.at[0], sems.at[1]),
        pltpu.make_async_copy(
            field_hbm.at[:, :, pl.ds(rows - tile, tile)], edges.at[1], sems.at[2]
        ),
        pltpu.make_async_copy(field_hbm.at[:, at], inner_ref, sems.at[3]),
        pltpu.make_async_copy(field_hbm.at[:, 1 - at], outer_ref, sems.at[4]),
    ]
    for copy in copies:
        copy.start()
    for copy in copies[:3]:
        copy.wait()
    for plane in range(CX):
        for side, row in enumerate((0, tile - 1)):
            for var in range(V):
                value = edges[side, var, plane, row : row + 1, :]
                scratch[plane * 2 + side, var : var + 1, :] = value
                to = side * V + var
                strips_ref[plane, to : to + 1, :] = value
    for group in range(send_ref.shape[0]):
        for slot in range(SLOT):
            send_ref[group, slot * V : (slot + 1) * V, :] = scratch[faces[slot, group]]
    for copy in copies[3:]:
        copy.wait()


def first_part(faces, field):
    groups, (rows, z) = faces.shape[1], field.shape[2:]
    return call(
        first_kernel,
        [f32(groups, SLOT * V, z), f32(CX, 2 * V, z), f32(V, rows, z), f32(V, rows, z)],
        [HBM, HBM],
        in_hbm(faces, field),
        scratch=[
            pltpu.SMEM(faces.shape, jnp.int32),
            pltpu.VMEM((2, V, CX, 8, z), jnp.float32),
            pltpu.VMEM((FACES, V, z), jnp.float32),
            pltpu.SemaphoreType.DMA((5,)),
        ],
    )


def patch_kernel(strips_ref, old_inner_ref, old_outer_ref, inner_ref, outer_ref):
    rows = inner_ref.shape[1]
    at = inner_plane()
    for ref, old, plane in (
        (inner_ref, old_inner_ref, at),
        (outer_ref, old_outer_ref, 1 - at),
    ):
        ref[...] = old[...]
        for side, row in enumerate(edge_rows(rows)):
            for var in range(V):
                here = side * V + var
                ref[var, row : row + 1, :] = strips_ref[plane, here : here + 1, :]


def patch_part(strips, inner, outer):
    shape = f32(*inner.shape)
    return call(patch_kernel, [shape, shape], [VMEM] * 3, (strips, inner, outer))


def setup_kernel(
    source_ref,
    live_ref,
    target_ref,
    stencil_ref,
    weight_ref,
    faces_hbm,
    right_hbm,
    conductivity_hbm,
    inverse_hbm,
    matrix_ref,
    mask_ref,
    coefs_ref,
    right_ref,
    conductivity_ref,
    inverse_ref,
    edge_ref,
    faces_ref,
    sems,
):
    copies = [
        pltpu.make_async_copy(faces_hbm, faces_ref, sems.at[0]),
        pltpu.make_async_copy(right_hbm, right_ref, sems.at[1]),
        pltpu.make_async_copy(conductivity_hbm, conductivity_ref, sems.at[2]),
        pltpu.make_async_copy(inverse_hbm, inverse_ref, sems.at[3]),
    ]
    for copy in copies:
        copy.start()
    entries = target_ref.shape[1]
    groups = mask_ref.shape[0]
    columns = matrix_ref.shape[1]
    row_ids = lax.broadcasted_iota(jnp.int32, (ROWS, entries), 0)
    entry_ids = lax.broadcasted_iota(jnp.int32, (ROWS, entries), 1)
    chosen = (row_ids // V == target_ref[...]) & (entry_ids < live_ref[0, 0])
    place = lax.broadcasted_iota(jnp.int32, (entries, columns), 0) + SLOT * source_ref[0, 0]
    place = jnp.where(place >= SLOT * groups, place - SLOT * groups, place)
    column_ids = lax.broadcasted_iota(jnp.int32, (entries, columns), 1)
    matrix = jnp.zeros((V * ROWS, columns), jnp.float32)
    for col in range(V):
        spread = jnp.concatenate(
            [jnp.where(chosen, weight_ref[var, col : col + 1, :], 0.0) for var in range(V)],
            axis=0,
        )
        order = (column_ids == place * V + col).astype(jnp.float32)
        matrix = matrix + jnp.dot(
            spread,
            order,
            precision=lax.Precision.HIGHEST,
            preferred_element_type=jnp.float32,
        )
    high = matrix.astype(jnp.bfloat16)
    matrix_ref[: V * ROWS, :] = high
    matrix_ref[V * ROWS :, :] = (matrix - high.astype(jnp.float32)).astype(jnp.bfloat16)
    for direction in range(6):
        for var in range(V):
            for col in range(V):
                coefs_ref[direction, var, col] = jnp.full(
                    coefs_ref.shape[3:], stencil_ref[var, col, direction], jnp.float32
                )
    copies[0].wait()
    tile_rows = lax.broadcasted_iota(jnp.int32, mask_ref.shape[1:], 0)
    for group in range(groups):
        mask_ref[group] = jnp.where(tile_rows < V, faces_ref[0, group], faces_ref[1, group])
    for copy in copies[1:]:
        copy.wait()
    for plane in range(CX):
        for side, row in enumerate(edge_rows(inverse_ref.shape[3])):
            for var in range(V):
                to = side * V + var
                for col in range(V):
                    edge_ref[col, plane, to : to + 1, :] = (
                        relax_weight * inverse_ref[var, col, plane, row : row + 1, :]
                    )


def setup_part(source, live, target, stencil, weight, faces, right, cond, inverse):
    groups, z = faces.shape[1], right.shape[-1]
    return call(
        setup_kernel,
        [
            jax.ShapeDtypeStruct((2 * V * ROWS, groups * SLOT * V), jnp.bfloat16),
            jax.ShapeDtypeStruct((groups, SLOT * V, z), jnp.int32),
            f32(6, V, V, 8, z),
            f32(*right.shape),
            f32(*cond.shape),
            f32(*inverse.shape),
            f32(V, CX, 2 * V, z),
        ],
        [SMEM, SMEM, VMEM, SMEM, VMEM, HBM, HBM, HBM, HBM],
        (source, live, target, stencil, weight, *in_hbm(faces, right, cond, inverse)),
        scratch=[pltpu.SMEM(faces.shape, jnp.int32), pltpu.SemaphoreType.DMA((4,))],
    )


def times(coef, value):
    rows, lanes = value.shape
    return (value.reshape(rows // 8, 8, lanes) * coef).reshape(rows, lanes)


def near_kernel(
    coefs_ref, inner_ref, outer_ref, right_ref, conductivity_ref, inner_load_ref, outer_load_ref
):
    rows, lanes = inner_ref.shape[1:]
    row_ids = lax.broadcasted_iota(jnp.int32, (rows, lanes), 0)
    lane_ids = lax.broadcasted_iota(jnp.int32, (rows, lanes), 1)
    at = inner_plane()
    for here, beside, plane, out_ref in (
        (inner_ref, outer_ref, at, inner_load_ref),
        (outer_ref, inner_ref, 1 - at, outer_load_ref),
    ):
        directions = (1 - plane, 2, 3, 4, 5)
        sums = [jnp.zeros((rows, lanes), jnp.float32) for _ in range(V)]
        for col in range(V):
            value = here[col]
            shifted = (
                beside[col],
                jnp.where(row_ids == 0, 0.0, pltpu.roll(value, 1, 0)),
                jnp.where(row_ids == rows - 1, 0.0, pltpu.roll(value, rows - 1, 0)),
                jnp.where(lane_ids == 0, 0.0, pltpu.roll(value, 1, 1)),
                jnp.where(lane_ids == lanes - 1, 0.0, pltpu.roll(value, lanes - 1, 1)),
            )
            for direction, moved in zip(directions, shifted):
                for var in range(V):
                    sums[var] = sums[var] + times(coefs_ref[direction, var, col], moved)
        cond = conductivity_ref[plane]
        for var in range(V):
            out_ref[var] = right_ref[var, plane] + cond * sums[var]


def near_part(coefs, inner, outer, right, cond):
    return call(
        near_kernel,
        [f32(*inner.shape), f32(*inner.shape)],
        [VMEM] * 5,
        (coefs, inner, outer, right, cond),
        flops=3_000_000,
        moved=1024 * 1024,
    )


def finish(plane, coefs_ref, here_ref, load_ref, outside_ref, conductivity_ref, inverse_ref):
    cond = conductivity_ref[plane]
    loads = []
    for var in range(V):
        total = times(coefs_ref[plane, var, 0], outside_ref[0])
        for col in range(1, V):
            total = total + times(coefs_ref[plane, var, col], outside_ref[col])
        loads.append(load_ref[var] + cond * total)
    values = []
    for var in range(V):
        total = inverse_ref[var, 0, plane] * loads[0]
        for col in range(1, V):
            total = total + inverse_ref[var, col, plane] * loads[col]
        values.append((1.0 - relax_weight) * here_ref[var] + relax_weight * total)
    return values


def outer_kernel(
    coefs_ref,
    here_ref,
    load_ref,
    outside_ref,
    conductivity_ref,
    inverse_ref,
    next_ref,
    strips_ref,
):
    plane = 1 - inner_plane()
    values = finish(
        plane, coefs_ref, here_ref, load_ref, outside_ref, conductivity_ref, inverse_ref
    )
    for var, value in enumerate(values):
        next_ref[var] = value
        for side, row in enumerate(edge_rows(value.shape[0])):
            to = side * V + var
            strips_ref[to : to + 1, :] = value[row : row + 1]


def outer_part(coefs, here, load, outside, cond, inverse):
    return call(
        outer_kernel,
        [f32(*here.shape), f32(2 * V, here.shape[-1])],
        [VMEM] * 6,
        (coefs, here, load, outside, cond, inverse),
        flops=1_000_000,
        moved=1024 * 1024,
    )


def inner_kernel(
    coefs_ref,
    here_ref,
    load_ref,
    outside_ref,
    conductivity_ref,
    inverse_ref,
    other_ref,
    next_ref,
    strips_ref,
):
    plane = inner_plane()
    strips_ref[1 - plane] = other_ref[...]
    values = finish(
        plane, coefs_ref, here_ref, load_ref, outside_ref, conductivity_ref, inverse_ref
    )
    for var, value in enumerate(values):
        next_ref[var] = value
        for side, row in enumerate(edge_rows(value.shape[0])):
            to = side * V + var
            strips_ref[plane, to : to + 1, :] = value[row : row + 1]


def inner_part(coefs, here, load, outside, cond, inverse, other):
    return call(
        inner_kernel,
        [f32(*here.shape), f32(CX, *other.shape)],
        [VMEM] * 7,
        (coefs, here, load, outside, cond, inverse, other),
        flops=1_000_000,
        moved=1024 * 1024,
    )


def new_strips(matrix_ref, edge_ref, strips_ref, got_ref):
    groups, block, z = got_ref.shape
    values = got_ref[...].reshape(groups * block, z)
    high = values.astype(jnp.bfloat16)
    low = (values - high.astype(jnp.float32)).astype(jnp.bfloat16)
    count = V * ROWS
    both = jnp.dot(matrix_ref[...], high, preferred_element_type=jnp.float32)
    rest = jnp.dot(matrix_ref[:count, :], low, preferred_element_type=jnp.float32)
    added = both[:count] + (both[count:] + rest)
    tiles = []
    for plane in range(CX):
        total = strips_ref[plane]
        for col in range(V):
            begin = col * ROWS + plane * 2 * V
            total = total + edge_ref[col, plane] * added[begin : begin + 2 * V]
        tiles.append(total)
    return tiles


def strip_kernel(
    matrix_ref, edge_ref, strips_ref, got_ref, mask_ref, send_ref, new_ref
):
    tiles = new_strips(matrix_ref, edge_ref, strips_ref, got_ref)
    upper = lax.broadcasted_iota(jnp.int32, tiles[0].shape, 0) < V
    faces = []
    for plane, tile in enumerate(tiles):
        new_ref[plane] = tile
        other = pltpu.roll(tile, V, 0)
        faces += [jnp.where(upper, tile, other), jnp.where(upper, other, tile)]
    for group in range(send_ref.shape[0]):
        mask = mask_ref[group]
        value = faces[FACES - 1]
        for face in range(FACES - 1):
            value = jnp.where(mask == face, faces[face], value)
        send_ref[group] = value


def strip_part(matrix, edge, strips, got, mask):
    return call(
        strip_kernel,
        [f32(*got.shape), f32(*strips.shape)],
        [VMEM] * 5,
        (matrix, edge, strips, got, mask),
    )


def last_kernel(
    matrix_ref, edge_ref, strips_ref, got_ref, inner_ref, outer_ref, out_ref
):
    rows = inner_ref.shape[1]
    at = inner_plane()
    for ref, plane in ((inner_ref, at), (outer_ref, 1 - at)):
        for var in range(V):
            out_ref[var, plane] = ref[var]
    tiles = new_strips(matrix_ref, edge_ref, strips_ref, got_ref)
    for plane, tile in enumerate(tiles):
        for side, row in enumerate(edge_rows(rows)):
            for var in range(V):
                here = side * V + var
                out_ref[var, plane, row : row + 1, :] = tile[here : here + 1]


def last_part(matrix, edge, strips, got, inner, outer):
    return call(
        last_kernel,
        f32(V, CX, *inner.shape[1:]),
        [VMEM] * 6,
        (matrix, edge, strips, got, inner, outer),
    )


def per_device(
    right_side,
    initial,
    block_inverse,
    conductivity,
    stencil,
    coupling_source,
    coupling_target,
    coupling_weight,
    live_count,
    send_faces,
):
    field = initial[0]
    right = right_side[0]
    inverse = block_inverse[0]
    cond = conductivity[0]
    coefs = jnp.transpose(stencil[0], (1, 2, 0))
    weight = jnp.transpose(coupling_weight[0, 0], (1, 2, 0))
    faces = jnp.transpose(send_faces[0, 0], (1, 0))

    count = lax.axis_size("within")
    core_swap = [(i, i ^ 1) for i in range(count)]
    chip_swap = [(i, i + 1) for i in range(1, count - 1, 2)]
    chip_swap += [(j, i) for i, j in chip_swap]

    send, new, inner, outer = first_part(faces, field)
    matrix, mask, coefs, right, cond, inverse, edge = setup_part(
        coupling_source[0],
        live_count,
        coupling_target[0],
        coefs,
        weight,
        faces,
        right,
        cond,
        inverse,
    )
    for sweep in range(SWEEPS):
        got = lax.all_to_all(send, "dom", 0, 0, tiled=True)
        inner, outer = patch_part(new, inner, outer)
        from_chip = lax.ppermute(outer, "within", chip_swap)
        from_core = lax.ppermute(inner, "within", core_swap)
        inner_load, outer_load = near_part(coefs, inner, outer, right, cond)
        outer, rows = outer_part(coefs, outer, outer_load, from_chip, cond, inverse)
        inner, strips = inner_part(coefs, inner, inner_load, from_core, cond, inverse, rows)
        if sweep < SWEEPS - 1:
            send, new = strip_part(matrix, edge, strips, got, mask)
        else:
            out = last_part(matrix, edge, strips, got, inner, outer)
    return out[None]


def solution(mesh):
    in_specs = (
        P("dom", None, "within", None, None),
        P("dom", None, "within", None, None),
        P("dom", None, None, "within", None, None),
        P("dom", "within", None, None),
        P("dom", None, None, None),
        P("dom", "within", None),
        P("dom", "within", None),
        P("dom", "within", None, None, None),
        P("dom", "within"),
        P("dom", "within", None, None),
    )
    out_specs = P("dom", None, "within", None, None)
    return jax.shard_map(
        per_device, mesh=mesh, in_specs=in_specs, out_specs=out_specs, check_vma=False
    )
```

```python
import functools

import jax
import jax.numpy as jnp
from jax import lax
from jax.experimental import pallas as pl
from jax.experimental.pallas import tpu as pltpu
from jax.sharding import PartitionSpec as P

SWEEPS = 3
V = 4
CX = 2
FACES = 4
SLOT = 2
ROWS = FACES * V
PIECES = 4

relax_weight = 0.8

VMEM = pl.BlockSpec(memory_space=pltpu.VMEM)
SMEM = pl.BlockSpec(memory_space=pltpu.SMEM)
HBM = pl.BlockSpec(memory_space=pltpu.HBM)
PARAMS = pltpu.CompilerParams(vmem_limit_bytes=24 * 1024 * 1024)


def call(
    kernel, out_shape, in_specs, args, out_specs=None, scratch=(), flops=0, moved=512 * 1024
):
    return pl.pallas_call(
        kernel,
        out_shape=out_shape,
        in_specs=in_specs,
        out_specs=out_specs or [VMEM] * len(out_shape),
        scratch_shapes=list(scratch),
        compiler_params=PARAMS,
        cost_estimate=pl.CostEstimate(flops=flops, bytes_accessed=moved, transcendentals=0),
    )(*args)


def in_hbm(*arrays):
    return tuple(pltpu.with_memory_space_constraint(array, pltpu.HBM) for array in arrays)


def f32(*shape):
    return jax.ShapeDtypeStruct(shape, jnp.float32)


def inner_plane():
    return 1 - lax.rem(lax.axis_index("within"), 2)


def edge_rows(rows):
    return (0, rows - 1)


def face_halves(tiles):
    upper = lax.broadcasted_iota(jnp.int32, tiles[0].shape, 0) < V
    above, below = [], []
    for tile in tiles:
        other = pltpu.roll(tile, V, 0)
        above += [tile, other]
        below += [other, tile]
    return upper, above, below


def send_pieces(block, send_hbm, sems, fill):
    pieces = sems.shape[0]
    size = block.shape[0] // pieces
    copies = []
    for piece in range(pieces):
        for group in range(piece * size, (piece + 1) * size):
            block[group] = fill(group)
        part = pl.ds(piece * size, size)
        copies.append(pltpu.make_async_copy(block.at[part], send_hbm.at[part], sems.at[piece]))
        copies[-1].start()
    return copies


def first_kernel(
    faces_hbm,
    field_hbm,
    send_hbm,
    strips_ref,
    inner_ref,
    outer_ref,
    faces,
    edges,
    choices,
    block,
    sems,
    send_sems,
):
    rows = field_hbm.shape[2]
    tile = edges.shape[3]
    at = inner_plane()
    copies = [
        pltpu.make_async_copy(faces_hbm, faces, sems.at[0]),
        pltpu.make_async_copy(field_hbm.at[:, :, pl.ds(0, tile)], edges.at[0], sems.at[1]),
        pltpu.make_async_copy(
            field_hbm.at[:, :, pl.ds(rows - tile, tile)], edges.at[1], sems.at[2]
        ),
        pltpu.make_async_copy(field_hbm.at[:, at], inner_ref, sems.at[3]),
        pltpu.make_async_copy(field_hbm.at[:, 1 - at], outer_ref, sems.at[4]),
    ]
    for copy in copies:
        copy.start()
    for copy in copies[:3]:
        copy.wait()
    for plane in range(CX):
        for side, row in enumerate((0, tile - 1)):
            for var in range(V):
                to = side * V + var
                strips_ref[plane, to : to + 1, :] = edges[side, var, plane, row : row + 1, :]
    upper, above, below = face_halves([strips_ref[plane] for plane in range(CX)])
    for face in range(FACES):
        for other in range(FACES):
            choices[face * FACES + other] = jnp.where(upper, above[face], below[other])

    def fill(group):
        return choices[faces[0, group] * FACES + faces[1, group]]

    for copy in send_pieces(block, send_hbm, send_sems, fill) + copies[3:]:
        copy.wait()


def first_part(faces, field):
    groups, (rows, z) = faces.shape[1], field.shape[2:]
    shape = (groups, SLOT * V, z)
    return call(
        first_kernel,
        [f32(*shape), f32(CX, 2 * V, z), f32(V, rows, z), f32(V, rows, z)],
        [HBM, HBM],
        in_hbm(faces, field),
        out_specs=[HBM, VMEM, VMEM, VMEM],
        scratch=[
            pltpu.SMEM(faces.shape, jnp.int32),
            pltpu.VMEM((2, V, CX, 8, z), jnp.float32),
            pltpu.VMEM((FACES * FACES, SLOT * V, z), jnp.float32),
            pltpu.VMEM(shape, jnp.float32),
            pltpu.SemaphoreType.DMA((5,)),
            pltpu.SemaphoreType.DMA((PIECES,)),
        ],
    )


def patch_kernel(strips_ref, old_inner_ref, old_outer_ref, inner_ref, outer_ref):
    rows = inner_ref.shape[1]
    at = inner_plane()
    for ref, old, plane in (
        (inner_ref, old_inner_ref, at),
        (outer_ref, old_outer_ref, 1 - at),
    ):
        ref[...] = old[...]
        for side, row in enumerate(edge_rows(rows)):
            for var in range(V):
                here = side * V + var
                ref[var, row : row + 1, :] = strips_ref[plane, here : here + 1, :]


def patch_part(strips, inner, outer):
    shape = f32(*inner.shape)
    return call(patch_kernel, [shape, shape], [VMEM] * 3, (strips, inner, outer))


def setup_kernel(
    live_ref,
    source_hbm,
    faces_hbm,
    stencil_hbm,
    target_hbm,
    weight_hbm,
    right_hbm,
    conductivity_hbm,
    inverse_hbm,
    matrix_ref,
    mask_ref,
    coefs_ref,
    right_ref,
    conductivity_ref,
    inverse_ref,
    edge_ref,
    source_ref,
    faces_ref,
    stencil_ref,
    target_ref,
    weight_ref,
    sems,
):
    pairs = (
        (source_hbm, source_ref),
        (faces_hbm, faces_ref),
        (stencil_hbm, stencil_ref),
        (target_hbm, target_ref),
        (weight_hbm, weight_ref),
        (right_hbm, right_ref),
        (conductivity_hbm, conductivity_ref),
        (inverse_hbm, inverse_ref),
    )
    copies = [
        pltpu.make_async_copy(here, there, sems.at[at]) for at, (here, there) in enumerate(pairs)
    ]
    for copy in copies:
        copy.start()
    for copy in copies[:5]:
        copy.wait()
    entries = target_ref.shape[1]
    groups = mask_ref.shape[0]
    columns = matrix_ref.shape[1]
    row_ids = lax.broadcasted_iota(jnp.int32, (ROWS, entries), 0)
    entry_ids = lax.broadcasted_iota(jnp.int32, (ROWS, entries), 1)
    chosen = (row_ids // V == target_ref[...]) & (entry_ids < live_ref[0, 0])
    place = lax.broadcasted_iota(jnp.int32, (entries, columns), 0) + SLOT * source_ref[0, 0]
    place = jnp.where(place >= SLOT * groups, place - SLOT * groups, place)
    shift = lax.broadcasted_iota(jnp.int32, (entries, columns), 1) - place * V
    matrix = jnp.zeros(matrix_ref.shape, jnp.float32)
    for col in range(V):
        spread = jnp.concatenate(
            [jnp.where(chosen, weight_ref[var, col : col + 1, :], 0.0) for var in range(V)],
            axis=0,
        )
        high = spread.astype(jnp.bfloat16)
        low = (spread - high.astype(jnp.float32)).astype(jnp.bfloat16)
        order = (shift == col).astype(jnp.float32).astype(jnp.bfloat16)
        matrix = matrix + jnp.dot(
            jnp.concatenate([high, low], axis=0), order, preferred_element_type=jnp.float32
        )
    matrix_ref[...] = matrix.astype(jnp.bfloat16)
    for direction in range(6):
        for var in range(V):
            for col in range(V):
                coefs_ref[direction, var, col] = jnp.full(
                    coefs_ref.shape[3:], stencil_ref[var, col, direction], jnp.float32
                )
    upper = lax.broadcasted_iota(jnp.int32, mask_ref.shape[1:], 0) < V
    for group in range(groups):
        mask_ref[group] = jnp.where(upper, faces_ref[0, group], faces_ref[1, group])
    for copy in copies[5:]:
        copy.wait()
    for plane in range(CX):
        for side, row in enumerate(edge_rows(inverse_ref.shape[3])):
            for var in range(V):
                to = side * V + var
                for col in range(V):
                    edge_ref[col, plane, to : to + 1, :] = (
                        relax_weight * inverse_ref[var, col, plane, row : row + 1, :]
                    )


def setup_part(live, source, faces, stencil, target, weight, right, cond, inverse):
    groups, z = faces.shape[1], right.shape[-1]
    scalars = [pltpu.SMEM(array.shape, array.dtype) for array in (source, faces, stencil)]
    vectors = [pltpu.VMEM(array.shape, array.dtype) for array in (target, weight)]
    return call(
        setup_kernel,
        [
            jax.ShapeDtypeStruct((2 * V * ROWS, groups * SLOT * V), jnp.bfloat16),
            jax.ShapeDtypeStruct((groups, SLOT * V, z), jnp.int32),
            f32(6, V, V, 8, z),
            f32(*right.shape),
            f32(*cond.shape),
            f32(*inverse.shape),
            f32(V, CX, 2 * V, z),
        ],
        [SMEM] + [HBM] * 8,
        (live, *in_hbm(source, faces, stencil, target, weight, right, cond, inverse)),
        scratch=[*scalars, *vectors, pltpu.SemaphoreType.DMA((8,))],
    )


def times(coef, value):
    rows, lanes = value.shape
    return (value.reshape(rows // 8, 8, lanes) * coef).reshape(rows, lanes)


def near_kernel(
    coefs_ref, inner_ref, outer_ref, right_ref, conductivity_ref, inner_load_ref, outer_load_ref
):
    rows, lanes = inner_ref.shape[1:]
    row_ids = lax.broadcasted_iota(jnp.int32, (rows, lanes), 0)
    lane_ids = lax.broadcasted_iota(jnp.int32, (rows, lanes), 1)
    at = inner_plane()
    for here, beside, plane, out_ref in (
        (inner_ref, outer_ref, at, inner_load_ref),
        (outer_ref, inner_ref, 1 - at, outer_load_ref),
    ):
        directions = (1 - plane, 2, 3, 4, 5)
        sums = [jnp.zeros((rows, lanes), jnp.float32) for _ in range(V)]
        for col in range(V):
            value = here[col]
            shifted = (
                beside[col],
                jnp.where(row_ids == 0, 0.0, pltpu.roll(value, 1, 0)),
                jnp.where(row_ids == rows - 1, 0.0, pltpu.roll(value, rows - 1, 0)),
                jnp.where(lane_ids == 0, 0.0, pltpu.roll(value, 1, 1)),
                jnp.where(lane_ids == lanes - 1, 0.0, pltpu.roll(value, lanes - 1, 1)),
            )
            for direction, moved in zip(directions, shifted):
                for var in range(V):
                    sums[var] = sums[var] + times(coefs_ref[direction, var, col], moved)
        cond = conductivity_ref[plane]
        for var in range(V):
            out_ref[var] = right_ref[var, plane] + cond * sums[var]


def near_part(coefs, inner, outer, right, cond):
    return call(
        near_kernel,
        [f32(*inner.shape), f32(*inner.shape)],
        [VMEM] * 5,
        (coefs, inner, outer, right, cond),
        flops=3_000_000,
        moved=1024 * 1024,
    )


def finish(plane, coefs_ref, here_ref, load_ref, outside_ref, conductivity_ref, inverse_ref):
    cond = conductivity_ref[plane]
    loads = []
    for var in range(V):
        total = times(coefs_ref[plane, var, 0], outside_ref[0])
        for col in range(1, V):
            total = total + times(coefs_ref[plane, var, col], outside_ref[col])
        loads.append(load_ref[var] + cond * total)
    values = []
    for var in range(V):
        total = inverse_ref[var, 0, plane] * loads[0]
        for col in range(1, V):
            total = total + inverse_ref[var, col, plane] * loads[col]
        values.append((1.0 - relax_weight) * here_ref[var] + relax_weight * total)
    return values


def outer_kernel(
    coefs_ref,
    here_ref,
    load_ref,
    outside_ref,
    conductivity_ref,
    inverse_ref,
    next_ref,
    strips_ref,
):
    plane = 1 - inner_plane()
    values = finish(
        plane, coefs_ref, here_ref, load_ref, outside_ref, conductivity_ref, inverse_ref
    )
    for var, value in enumerate(values):
        next_ref[var] = value
        for side, row in enumerate(edge_rows(value.shape[0])):
            to = side * V + var
            strips_ref[to : to + 1, :] = value[row : row + 1]


def outer_part(coefs, here, load, outside, cond, inverse):
    return call(
        outer_kernel,
        [f32(*here.shape), f32(2 * V, here.shape[-1])],
        [VMEM] * 6,
        (coefs, here, load, outside, cond, inverse),
        flops=1_000_000,
        moved=1024 * 1024,
    )


def inner_kernel(
    coefs_ref,
    here_ref,
    load_ref,
    outside_ref,
    conductivity_ref,
    inverse_ref,
    other_ref,
    next_ref,
    strips_ref,
):
    plane = inner_plane()
    strips_ref[1 - plane] = other_ref[...]
    values = finish(
        plane, coefs_ref, here_ref, load_ref, outside_ref, conductivity_ref, inverse_ref
    )
    for var, value in enumerate(values):
        next_ref[var] = value
        for side, row in enumerate(edge_rows(value.shape[0])):
            to = side * V + var
            strips_ref[plane, to : to + 1, :] = value[row : row + 1]


def inner_part(coefs, here, load, outside, cond, inverse, other):
    return call(
        inner_kernel,
        [f32(*here.shape), f32(CX, *other.shape)],
        [VMEM] * 7,
        (coefs, here, load, outside, cond, inverse, other),
        flops=1_000_000,
        moved=1024 * 1024,
    )


def new_strips(matrix_ref, edge_ref, strips_ref, got_ref):
    groups, block, z = got_ref.shape
    values = got_ref[...].reshape(groups * block, z)
    high = values.astype(jnp.bfloat16)
    low = (values - high.astype(jnp.float32)).astype(jnp.bfloat16)
    count = V * ROWS
    both = jnp.dot(matrix_ref[...], high, preferred_element_type=jnp.float32)
    rest = jnp.dot(matrix_ref[:count, :], low, preferred_element_type=jnp.float32)
    added = both[:count] + (both[count:] + rest)
    tiles = []
    for plane in range(CX):
        total = strips_ref[plane]
        for col in range(V):
            begin = col * ROWS + plane * 2 * V
            total = total + edge_ref[col, plane] * added[begin : begin + 2 * V]
        tiles.append(total)
    return tiles


def strip_kernel(
    matrix_ref, edge_ref, strips_ref, got_ref, mask_ref, send_hbm, new_ref, block, sems
):
    tiles = new_strips(matrix_ref, edge_ref, strips_ref, got_ref)
    for plane, tile in enumerate(tiles):
        new_ref[plane] = tile
    upper, above, below = face_halves(tiles)
    faces = [jnp.where(upper, above[face], below[face]) for face in range(FACES)]

    def fill(group):
        mask = mask_ref[group]
        value = faces[FACES - 1]
        for face in range(FACES - 1):
            value = jnp.where(mask == face, faces[face], value)
        return value

    for copy in send_pieces(block, send_hbm, sems, fill):
        copy.wait()


def strip_part(matrix, edge, strips, got, mask):
    return call(
        strip_kernel,
        [f32(*got.shape), f32(*strips.shape)],
        [VMEM] * 5,
        (matrix, edge, strips, got, mask),
        out_specs=[HBM, VMEM],
        scratch=[pltpu.VMEM(got.shape, jnp.float32), pltpu.SemaphoreType.DMA((PIECES,))],
    )


def last_kernel(
    matrix_ref, edge_ref, strips_ref, got_ref, inner_ref, outer_ref, out_hbm, edges, sems
):
    rows = inner_ref.shape[1]
    tile = edges.shape[3]
    at = inner_plane()
    middle = pl.ds(tile, rows - 2 * tile)
    copies = [
        pltpu.make_async_copy(
            ref.at[:, middle], out_hbm.at[:, plane, middle], sems.at[number]
        )
        for number, (ref, plane) in enumerate(((inner_ref, at), (outer_ref, 1 - at)))
    ]
    for copy in copies:
        copy.start()
    starts = (0, rows - tile)
    for ref, plane in ((inner_ref, at), (outer_ref, 1 - at)):
        for side, start in enumerate(starts):
            for var in range(V):
                edges[side, var, plane] = ref[var, start : start + tile, :]
    tiles = new_strips(matrix_ref, edge_ref, strips_ref, got_ref)
    for plane, value in enumerate(tiles):
        for side, row in enumerate((0, tile - 1)):
            for var in range(V):
                here = side * V + var
                edges[side, var, plane, row : row + 1, :] = value[here : here + 1]
    for side, start in enumerate(starts):
        copies.append(
            pltpu.make_async_copy(
                edges.at[side], out_hbm.at[:, :, pl.ds(start, tile)], sems.at[2 + side]
            )
        )
        copies[-1].start()
    for copy in copies:
        copy.wait()


def last_part(matrix, edge, strips, got, inner, outer):
    rows, z = inner.shape[1:]
    return call(
        last_kernel,
        [f32(V, CX, rows, z)],
        [VMEM] * 6,
        (matrix, edge, strips, got, inner, outer),
        out_specs=[HBM],
        scratch=[pltpu.VMEM((2, V, CX, 8, z), jnp.float32), pltpu.SemaphoreType.DMA((4,))],
    )[0]


def per_device(
    right_side,
    initial,
    block_inverse,
    conductivity,
    stencil,
    coupling_source,
    coupling_target,
    coupling_weight,
    live_count,
    send_faces,
):
    field = initial[0]
    right = right_side[0]
    inverse = block_inverse[0]
    cond = conductivity[0]
    coefs = jnp.transpose(stencil[0], (1, 2, 0))
    weight = jnp.transpose(coupling_weight[0, 0], (1, 2, 0))
    faces = jnp.transpose(send_faces[0, 0], (1, 0))

    count = lax.axis_size("within")
    core_swap = [(i, i ^ 1) for i in range(count)]
    chip_swap = [(i, i + 1) for i in range(1, count - 1, 2)]
    chip_swap += [(j, i) for i, j in chip_swap]

    send, new, inner, outer = first_part(faces, field)
    matrix, mask, coefs, right, cond, inverse, edge = setup_part(
        live_count,
        coupling_source[0],
        faces,
        coefs,
        coupling_target[0],
        weight,
        right,
        cond,
        inverse,
    )
    for sweep in range(SWEEPS):
        got = lax.all_to_all(send, "dom", 0, 0, tiled=True)
        inner, outer = patch_part(new, inner, outer)
        from_chip = lax.ppermute(outer, "within", chip_swap)
        from_core = lax.ppermute(inner, "within", core_swap)
        inner_load, outer_load = near_part(coefs, inner, outer, right, cond)
        outer, rows = outer_part(coefs, outer, outer_load, from_chip, cond, inverse)
        inner, strips = inner_part(coefs, inner, inner_load, from_core, cond, inverse, rows)
        if sweep < SWEEPS - 1:
            send, new = strip_part(matrix, edge, strips, got, mask)
        else:
            out = last_part(matrix, edge, strips, got, inner, outer)
    return out[None]


def solution(mesh):
    in_specs = (
        P("dom", None, "within", None, None),
        P("dom", None, "within", None, None),
        P("dom", None, None, "within", None, None),
        P("dom", "within", None, None),
        P("dom", None, None, None),
        P("dom", "within", None),
        P("dom", "within", None),
        P("dom", "within", None, None, None),
        P("dom", "within"),
        P("dom", "within", None, None),
    )
    out_specs = P("dom", None, "within", None, None)
    return jax.shard_map(
        per_device, mesh=mesh, in_specs=in_specs, out_specs=out_specs, check_vma=False
    )
```

```python
import functools

import jax
import jax.numpy as jnp
from jax import lax
from jax.experimental import pallas as pl
from jax.experimental.pallas import tpu as pltpu
from jax.sharding import PartitionSpec as P

SWEEPS = 3
V = 4
CX = 2
FACES = 4
SLOT = 2
ROWS = FACES * V
PIECES = 4

relax_weight = 0.8

VMEM = pl.BlockSpec(memory_space=pltpu.VMEM)
SMEM = pl.BlockSpec(memory_space=pltpu.SMEM)
HBM = pl.BlockSpec(memory_space=pltpu.HBM)
PARAMS = pltpu.CompilerParams(vmem_limit_bytes=24 * 1024 * 1024)


def call(
    kernel, out_shape, in_specs, args, out_specs=None, scratch=(), flops=0, moved=512 * 1024
):
    return pl.pallas_call(
        kernel,
        out_shape=out_shape,
        in_specs=in_specs,
        out_specs=out_specs or [VMEM] * len(out_shape),
        scratch_shapes=list(scratch),
        compiler_params=PARAMS,
        cost_estimate=pl.CostEstimate(flops=flops, bytes_accessed=moved, transcendentals=0),
    )(*args)


def in_hbm(*arrays):
    return tuple(pltpu.with_memory_space_constraint(array, pltpu.HBM) for array in arrays)


def f32(*shape):
    return jax.ShapeDtypeStruct(shape, jnp.float32)


def inner_plane():
    return 1 - lax.rem(lax.axis_index("within"), 2)


def edge_rows(rows):
    return (0, rows - 1)


def face_halves(tiles):
    upper = lax.broadcasted_iota(jnp.int32, tiles[0].shape, 0) < V
    above, below = [], []
    for tile in tiles:
        other = pltpu.roll(tile, V, 0)
        above += [tile, other]
        below += [other, tile]
    return upper, above, below


def send_pieces(block, send_hbm, sems, fill):
    pieces = sems.shape[0]
    size = block.shape[0] // pieces
    copies = []
    for piece in range(pieces):
        for place in range(piece * size, (piece + 1) * size):
            block[place] = fill(block.shape[0] - 1 - place)
        part = pl.ds(piece * size, size)
        copies.append(pltpu.make_async_copy(block.at[part], send_hbm.at[part], sems.at[piece]))
        copies[-1].start()
    return copies


def first_kernel(
    faces_hbm,
    field_hbm,
    send_hbm,
    strips_ref,
    inner_ref,
    outer_ref,
    faces,
    edges,
    choices,
    block,
    sems,
    send_sems,
):
    rows = field_hbm.shape[2]
    tile = edges.shape[3]
    at = inner_plane()
    copies = [
        pltpu.make_async_copy(faces_hbm, faces, sems.at[0]),
        pltpu.make_async_copy(field_hbm.at[:, :, pl.ds(0, tile)], edges.at[0], sems.at[1]),
        pltpu.make_async_copy(
            field_hbm.at[:, :, pl.ds(rows - tile, tile)], edges.at[1], sems.at[2]
        ),
        pltpu.make_async_copy(field_hbm.at[:, at], inner_ref, sems.at[3]),
        pltpu.make_async_copy(field_hbm.at[:, 1 - at], outer_ref, sems.at[4]),
    ]
    for copy in copies:
        copy.start()
    for copy in copies[:3]:
        copy.wait()
    for plane in range(CX):
        for side, row in enumerate((0, tile - 1)):
            for var in range(V):
                to = side * V + var
                strips_ref[plane, to : to + 1, :] = edges[side, var, plane, row : row + 1, :]
    upper, above, below = face_halves([strips_ref[plane] for plane in range(CX)])
    for face in range(FACES):
        for other in range(FACES):
            choices[face * FACES + other] = jnp.where(upper, above[face], below[other])

    def fill(group):
        return choices[faces[0, group] * FACES + faces[1, group]]

    for copy in send_pieces(block, send_hbm, send_sems, fill) + copies[3:]:
        copy.wait()


def first_part(faces, field):
    groups, (rows, z) = faces.shape[1], field.shape[2:]
    shape = (groups, SLOT * V, z)
    return call(
        first_kernel,
        [f32(*shape), f32(CX, 2 * V, z), f32(V, rows, z), f32(V, rows, z)],
        [HBM, HBM],
        in_hbm(faces, field),
        out_specs=[HBM, VMEM, VMEM, VMEM],
        scratch=[
            pltpu.SMEM(faces.shape, jnp.int32),
            pltpu.VMEM((2, V, CX, 8, z), jnp.float32),
            pltpu.VMEM((FACES * FACES, SLOT * V, z), jnp.float32),
            pltpu.VMEM(shape, jnp.float32),
            pltpu.SemaphoreType.DMA((5,)),
            pltpu.SemaphoreType.DMA((PIECES,)),
        ],
    )


def patch_kernel(strips_ref, old_inner_ref, old_outer_ref, inner_ref, outer_ref):
    rows = inner_ref.shape[1]
    at = inner_plane()
    for ref, old, plane in (
        (inner_ref, old_inner_ref, at),
        (outer_ref, old_outer_ref, 1 - at),
    ):
        ref[...] = old[...]
        for side, row in enumerate(edge_rows(rows)):
            for var in range(V):
                here = side * V + var
                ref[var, row : row + 1, :] = strips_ref[plane, here : here + 1, :]


def patch_part(strips, inner, outer):
    shape = f32(*inner.shape)
    return call(patch_kernel, [shape, shape], [VMEM] * 3, (strips, inner, outer))


def setup_kernel(
    live_ref,
    source_hbm,
    faces_hbm,
    stencil_hbm,
    target_hbm,
    weight_hbm,
    right_hbm,
    conductivity_hbm,
    inverse_hbm,
    matrix_ref,
    mask_ref,
    coefs_ref,
    right_ref,
    conductivity_ref,
    inverse_ref,
    edge_ref,
    source_ref,
    faces_ref,
    stencil_ref,
    target_ref,
    weight_ref,
    sems,
):
    pairs = (
        (source_hbm, source_ref),
        (faces_hbm, faces_ref),
        (stencil_hbm, stencil_ref),
        (target_hbm, target_ref),
        (weight_hbm, weight_ref),
        (right_hbm, right_ref),
        (conductivity_hbm, conductivity_ref),
        (inverse_hbm, inverse_ref),
    )
    copies = [
        pltpu.make_async_copy(here, there, sems.at[at]) for at, (here, there) in enumerate(pairs)
    ]
    for copy in copies:
        copy.start()
    for copy in copies[:5]:
        copy.wait()
    entries = target_ref.shape[1]
    groups = mask_ref.shape[0]
    columns = matrix_ref.shape[1]
    row_ids = lax.broadcasted_iota(jnp.int32, (ROWS, entries), 0)
    entry_ids = lax.broadcasted_iota(jnp.int32, (ROWS, entries), 1)
    chosen = (row_ids // V == target_ref[...]) & (entry_ids < live_ref[0, 0])
    place = lax.broadcasted_iota(jnp.int32, (entries, columns), 0) + SLOT * source_ref[0, 0]
    place = jnp.where(place >= SLOT * groups, place - SLOT * groups, place)
    place = SLOT * (groups - 1 - place // SLOT) + lax.rem(place, SLOT)
    shift = lax.broadcasted_iota(jnp.int32, (entries, columns), 1) - place * V
    matrix = jnp.zeros(matrix_ref.shape, jnp.float32)
    for col in range(V):
        spread = jnp.concatenate(
            [jnp.where(chosen, weight_ref[var, col : col + 1, :], 0.0) for var in range(V)],
            axis=0,
        )
        high = spread.astype(jnp.bfloat16)
        low = (spread - high.astype(jnp.float32)).astype(jnp.bfloat16)
        order = (shift == col).astype(jnp.float32).astype(jnp.bfloat16)
        matrix = matrix + jnp.dot(
            jnp.concatenate([high, low], axis=0), order, preferred_element_type=jnp.float32
        )
    matrix_ref[...] = matrix.astype(jnp.bfloat16)
    for direction in range(6):
        for var in range(V):
            for col in range(V):
                coefs_ref[direction, var, col] = jnp.full(
                    coefs_ref.shape[3:], stencil_ref[var, col, direction], jnp.float32
                )
    upper = lax.broadcasted_iota(jnp.int32, mask_ref.shape[1:], 0) < V
    for group in range(groups):
        mask_ref[group] = jnp.where(upper, faces_ref[0, group], faces_ref[1, group])
    for copy in copies[5:]:
        copy.wait()
    for plane in range(CX):
        for side, row in enumerate(edge_rows(inverse_ref.shape[3])):
            for var in range(V):
                to = side * V + var
                for col in range(V):
                    edge_ref[col, plane, to : to + 1, :] = (
                        relax_weight * inverse_ref[var, col, plane, row : row + 1, :]
                    )


def setup_part(live, source, faces, stencil, target, weight, right, cond, inverse):
    groups, z = faces.shape[1], right.shape[-1]
    scalars = [pltpu.SMEM(array.shape, array.dtype) for array in (source, faces, stencil)]
    vectors = [pltpu.VMEM(array.shape, array.dtype) for array in (target, weight)]
    return call(
        setup_kernel,
        [
            jax.ShapeDtypeStruct((2 * V * ROWS, groups * SLOT * V), jnp.bfloat16),
            jax.ShapeDtypeStruct((groups, SLOT * V, z), jnp.int32),
            f32(6, V, V, 8, z),
            f32(*right.shape),
            f32(*cond.shape),
            f32(*inverse.shape),
            f32(V, CX, 2 * V, z),
        ],
        [SMEM] + [HBM] * 8,
        (live, *in_hbm(source, faces, stencil, target, weight, right, cond, inverse)),
        scratch=[*scalars, *vectors, pltpu.SemaphoreType.DMA((8,))],
    )


def times(coef, value):
    rows, lanes = value.shape
    return (value.reshape(rows // 8, 8, lanes) * coef).reshape(rows, lanes)


def near_kernel(
    coefs_ref, inner_ref, outer_ref, right_ref, conductivity_ref, inner_load_ref, outer_load_ref
):
    rows, lanes = inner_ref.shape[1:]
    row_ids = lax.broadcasted_iota(jnp.int32, (rows, lanes), 0)
    lane_ids = lax.broadcasted_iota(jnp.int32, (rows, lanes), 1)
    at = inner_plane()
    for here, beside, plane, out_ref in (
        (inner_ref, outer_ref, at, inner_load_ref),
        (outer_ref, inner_ref, 1 - at, outer_load_ref),
    ):
        directions = (1 - plane, 2, 3, 4, 5)
        sums = [jnp.zeros((rows, lanes), jnp.float32) for _ in range(V)]
        for col in range(V):
            value = here[col]
            shifted = (
                beside[col],
                jnp.where(row_ids == 0, 0.0, pltpu.roll(value, 1, 0)),
                jnp.where(row_ids == rows - 1, 0.0, pltpu.roll(value, rows - 1, 0)),
                jnp.where(lane_ids == 0, 0.0, pltpu.roll(value, 1, 1)),
                jnp.where(lane_ids == lanes - 1, 0.0, pltpu.roll(value, lanes - 1, 1)),
            )
            for direction, moved in zip(directions, shifted):
                for var in range(V):
                    sums[var] = sums[var] + times(coefs_ref[direction, var, col], moved)
        cond = conductivity_ref[plane]
        for var in range(V):
            out_ref[var] = right_ref[var, plane] + cond * sums[var]


def near_part(coefs, inner, outer, right, cond):
    return call(
        near_kernel,
        [f32(*inner.shape), f32(*inner.shape)],
        [VMEM] * 5,
        (coefs, inner, outer, right, cond),
        flops=3_000_000,
        moved=1024 * 1024,
    )


def finish(plane, coefs_ref, here_ref, load_ref, outside_ref, conductivity_ref, inverse_ref):
    cond = conductivity_ref[plane]
    loads = []
    for var in range(V):
        total = times(coefs_ref[plane, var, 0], outside_ref[0])
        for col in range(1, V):
            total = total + times(coefs_ref[plane, var, col], outside_ref[col])
        loads.append(load_ref[var] + cond * total)
    values = []
    for var in range(V):
        total = inverse_ref[var, 0, plane] * loads[0]
        for col in range(1, V):
            total = total + inverse_ref[var, col, plane] * loads[col]
        values.append((1.0 - relax_weight) * here_ref[var] + relax_weight * total)
    return values


def outer_kernel(
    coefs_ref,
    here_ref,
    load_ref,
    outside_ref,
    conductivity_ref,
    inverse_ref,
    next_ref,
    strips_ref,
):
    plane = 1 - inner_plane()
    values = finish(
        plane, coefs_ref, here_ref, load_ref, outside_ref, conductivity_ref, inverse_ref
    )
    for var, value in enumerate(values):
        next_ref[var] = value
        for side, row in enumerate(edge_rows(value.shape[0])):
            to = side * V + var
            strips_ref[to : to + 1, :] = value[row : row + 1]


def outer_part(coefs, here, load, outside, cond, inverse):
    return call(
        outer_kernel,
        [f32(*here.shape), f32(2 * V, here.shape[-1])],
        [VMEM] * 6,
        (coefs, here, load, outside, cond, inverse),
        flops=1_000_000,
        moved=1024 * 1024,
    )


def inner_kernel(
    coefs_ref,
    here_ref,
    load_ref,
    outside_ref,
    conductivity_ref,
    inverse_ref,
    other_ref,
    next_ref,
    strips_ref,
):
    plane = inner_plane()
    strips_ref[1 - plane] = other_ref[...]
    values = finish(
        plane, coefs_ref, here_ref, load_ref, outside_ref, conductivity_ref, inverse_ref
    )
    for var, value in enumerate(values):
        next_ref[var] = value
        for side, row in enumerate(edge_rows(value.shape[0])):
            to = side * V + var
            strips_ref[plane, to : to + 1, :] = value[row : row + 1]


def inner_part(coefs, here, load, outside, cond, inverse, other):
    return call(
        inner_kernel,
        [f32(*here.shape), f32(CX, *other.shape)],
        [VMEM] * 7,
        (coefs, here, load, outside, cond, inverse, other),
        flops=1_000_000,
        moved=1024 * 1024,
    )


def new_strips(matrix_ref, edge_ref, strips_ref, got_ref):
    groups, block, z = got_ref.shape
    values = got_ref[...].reshape(groups * block, z)
    high = values.astype(jnp.bfloat16)
    low = (values - high.astype(jnp.float32)).astype(jnp.bfloat16)
    count = V * ROWS
    both = jnp.dot(matrix_ref[...], high, preferred_element_type=jnp.float32)
    rest = jnp.dot(matrix_ref[:count, :], low, preferred_element_type=jnp.float32)
    added = both[:count] + (both[count:] + rest)
    tiles = []
    for plane in range(CX):
        total = strips_ref[plane]
        for col in range(V):
            begin = col * ROWS + plane * 2 * V
            total = total + edge_ref[col, plane] * added[begin : begin + 2 * V]
        tiles.append(total)
    return tiles


def strip_kernel(
    matrix_ref, edge_ref, strips_ref, got_ref, mask_ref, send_hbm, new_ref, block, sems
):
    tiles = new_strips(matrix_ref, edge_ref, strips_ref, got_ref)
    for plane, tile in enumerate(tiles):
        new_ref[plane] = tile
    upper, above, below = face_halves(tiles)
    faces = [jnp.where(upper, above[face], below[face]) for face in range(FACES)]

    def fill(group):
        mask = mask_ref[group]
        value = faces[FACES - 1]
        for face in range(FACES - 1):
            value = jnp.where(mask == face, faces[face], value)
        return value

    for copy in send_pieces(block, send_hbm, sems, fill):
        copy.wait()


def strip_part(matrix, edge, strips, got, mask):
    return call(
        strip_kernel,
        [f32(*got.shape), f32(*strips.shape)],
        [VMEM] * 5,
        (matrix, edge, strips, got, mask),
        out_specs=[HBM, VMEM],
        scratch=[pltpu.VMEM(got.shape, jnp.float32), pltpu.SemaphoreType.DMA((PIECES,))],
    )


def last_kernel(
    matrix_ref, edge_ref, strips_ref, got_ref, inner_ref, outer_ref, out_hbm, edges, sems
):
    rows = inner_ref.shape[1]
    tile = edges.shape[3]
    at = inner_plane()
    middle = pl.ds(tile, rows - 2 * tile)
    copies = [
        pltpu.make_async_copy(
            ref.at[:, middle], out_hbm.at[:, plane, middle], sems.at[number]
        )
        for number, (ref, plane) in enumerate(((inner_ref, at), (outer_ref, 1 - at)))
    ]
    for copy in copies:
        copy.start()
    starts = (0, rows - tile)
    for ref, plane in ((inner_ref, at), (outer_ref, 1 - at)):
        for side, start in enumerate(starts):
            for var in range(V):
                edges[side, var, plane] = ref[var, start : start + tile, :]
    tiles = new_strips(matrix_ref, edge_ref, strips_ref, got_ref)
    for plane, value in enumerate(tiles):
        for side, row in enumerate((0, tile - 1)):
            for var in range(V):
                here = side * V + var
                edges[side, var, plane, row : row + 1, :] = value[here : here + 1]
    for side, start in enumerate(starts):
        copies.append(
            pltpu.make_async_copy(
                edges.at[side], out_hbm.at[:, :, pl.ds(start, tile)], sems.at[2 + side]
            )
        )
        copies[-1].start()
    for copy in copies:
        copy.wait()


def last_part(matrix, edge, strips, got, inner, outer):
    rows, z = inner.shape[1:]
    return call(
        last_kernel,
        [f32(V, CX, rows, z)],
        [VMEM] * 6,
        (matrix, edge, strips, got, inner, outer),
        out_specs=[HBM],
        scratch=[pltpu.VMEM((2, V, CX, 8, z), jnp.float32), pltpu.SemaphoreType.DMA((4,))],
    )[0]


def per_device(
    right_side,
    initial,
    block_inverse,
    conductivity,
    stencil,
    coupling_source,
    coupling_target,
    coupling_weight,
    live_count,
    send_faces,
):
    field = initial[0]
    right = right_side[0]
    inverse = block_inverse[0]
    cond = conductivity[0]
    coefs = jnp.transpose(stencil[0], (1, 2, 0))
    weight = jnp.transpose(coupling_weight[0, 0], (1, 2, 0))
    faces = jnp.transpose(send_faces[0, 0], (1, 0))

    count = lax.axis_size("within")
    core_swap = [(i, i ^ 1) for i in range(count)]
    chip_swap = [(i, i + 1) for i in range(1, count - 1, 2)]
    chip_swap += [(j, i) for i, j in chip_swap]

    send, new, inner, outer = first_part(faces, field)
    matrix, mask, coefs, right, cond, inverse, edge = setup_part(
        live_count,
        coupling_source[0],
        faces,
        coefs,
        coupling_target[0],
        weight,
        right,
        cond,
        inverse,
    )
    members = [list(reversed(range(lax.axis_size("dom"))))]
    for sweep in range(SWEEPS):
        got = lax.all_to_all(send, "dom", 0, 0, tiled=True, axis_index_groups=members)
        inner, outer = patch_part(new, inner, outer)
        from_chip = lax.ppermute(outer, "within", chip_swap)
        from_core = lax.ppermute(inner, "within", core_swap)
        inner_load, outer_load = near_part(coefs, inner, outer, right, cond)
        outer, rows = outer_part(coefs, outer, outer_load, from_chip, cond, inverse)
        inner, strips = inner_part(coefs, inner, inner_load, from_core, cond, inverse, rows)
        if sweep < SWEEPS - 1:
            send, new = strip_part(matrix, edge, strips, got, mask)
        else:
            out = last_part(matrix, edge, strips, got, inner, outer)
    return out[None]


def solution(mesh):
    in_specs = (
        P("dom", None, "within", None, None),
        P("dom", None, "within", None, None),
        P("dom", None, None, "within", None, None),
        P("dom", "within", None, None),
        P("dom", None, None, None),
        P("dom", "within", None),
        P("dom", "within", None),
        P("dom", "within", None, None, None),
        P("dom", "within"),
        P("dom", "within", None, None),
    )
    out_specs = P("dom", None, "within", None, None)
    return jax.shard_map(
        per_device, mesh=mesh, in_specs=in_specs, out_specs=out_specs, check_vma=False
    )
```

```python
import functools

import jax
import jax.numpy as jnp
from jax import lax
from jax.experimental import pallas as pl
from jax.experimental.pallas import tpu as pltpu
from jax.sharding import PartitionSpec as P

SWEEPS = 3
V = 4
CX = 2
FACES = 4
SLOT = 2
ROWS = FACES * V
PIECES = 4
STAGED = 6

relax_weight = 0.8

VMEM = pl.BlockSpec(memory_space=pltpu.VMEM)
SMEM = pl.BlockSpec(memory_space=pltpu.SMEM)
HBM = pl.BlockSpec(memory_space=pltpu.HBM)
PARAMS = pltpu.CompilerParams(vmem_limit_bytes=24 * 1024 * 1024)


def call(
    kernel, out_shape, in_specs, args, out_specs=None, scratch=(), flops=0, moved=512 * 1024
):
    return pl.pallas_call(
        kernel,
        out_shape=out_shape,
        in_specs=in_specs,
        out_specs=out_specs or [VMEM] * len(out_shape),
        scratch_shapes=list(scratch),
        compiler_params=PARAMS,
        cost_estimate=pl.CostEstimate(flops=flops, bytes_accessed=moved, transcendentals=0),
    )(*args)


def in_hbm(*arrays):
    return tuple(pltpu.with_memory_space_constraint(array, pltpu.HBM) for array in arrays)


def f32(*shape):
    return jax.ShapeDtypeStruct(shape, jnp.float32)


def inner_plane():
    return 1 - lax.rem(lax.axis_index("within"), 2)


def edge_rows(rows):
    return (0, rows - 1)


def face_halves(tiles):
    upper = lax.broadcasted_iota(jnp.int32, tiles[0].shape, 0) < V
    above, below = [], []
    for tile in tiles:
        other = pltpu.roll(tile, V, 0)
        above += [tile, other]
        below += [other, tile]
    return upper, above, below


def send_pieces(block, send_hbm, sems, fill):
    pieces = sems.shape[0]
    size = block.shape[0] // pieces
    copies = []
    for piece in range(pieces):
        for place in range(piece * size, (piece + 1) * size):
            block[place] = fill(block.shape[0] - 1 - place)
        part = pl.ds(piece * size, size)
        copies.append(pltpu.make_async_copy(block.at[part], send_hbm.at[part], sems.at[piece]))
        copies[-1].start()
    return copies


def first_kernel(
    faces_hbm,
    field_hbm,
    stencil_hbm,
    *refs,
):
    staged_hbm, refs = refs[:STAGED], refs[STAGED:]
    send_hbm, strips_ref, inner_ref, outer_ref, mask_ref, coefs_ref = refs[:6]
    staged, refs = refs[6 : 6 + STAGED], refs[6 + STAGED :]
    faces, stencil, edges, choices, block, sems, send_sems = refs
    rows = field_hbm.shape[2]
    tile = edges.shape[3]
    at = inner_plane()
    pairs = [
        (faces_hbm, faces),
        (field_hbm.at[:, :, pl.ds(0, tile)], edges.at[0]),
        (field_hbm.at[:, :, pl.ds(rows - tile, tile)], edges.at[1]),
        (stencil_hbm, stencil),
        (field_hbm.at[:, at], inner_ref),
        (field_hbm.at[:, 1 - at], outer_ref),
        *zip(staged_hbm, staged),
    ]
    copies = [
        pltpu.make_async_copy(here, there, sems.at[number])
        for number, (here, there) in enumerate(pairs)
    ]
    for copy in copies:
        copy.start()
    for copy in copies[:3]:
        copy.wait()
    for plane in range(CX):
        for side, row in enumerate((0, tile - 1)):
            for var in range(V):
                to = side * V + var
                strips_ref[plane, to : to + 1, :] = edges[side, var, plane, row : row + 1, :]
    upper, above, below = face_halves([strips_ref[plane] for plane in range(CX)])
    for face in range(FACES):
        for other in range(FACES):
            choices[face * FACES + other] = jnp.where(upper, above[face], below[other])

    def fill(group):
        return choices[faces[0, group] * FACES + faces[1, group]]

    sends = send_pieces(block, send_hbm, send_sems, fill)
    for group in range(mask_ref.shape[0]):
        mask_ref[group] = jnp.where(upper, faces[0, group], faces[1, group])
    copies[3].wait()
    for direction in range(6):
        for var in range(V):
            for col in range(V):
                coefs_ref[direction, var, col] = jnp.full(
                    coefs_ref.shape[3:], stencil[var, col, direction], jnp.float32
                )
    for copy in sends + copies[4:]:
        copy.wait()


def first_part(faces, field, stencil, *staged):
    groups, (rows, z) = faces.shape[1], field.shape[2:]
    shape = (groups, SLOT * V, z)
    return call(
        first_kernel,
        [
            f32(*shape),
            f32(CX, 2 * V, z),
            f32(V, rows, z),
            f32(V, rows, z),
            jax.ShapeDtypeStruct(shape, jnp.int32),
            f32(6, V, V, 8, z),
            *(jax.ShapeDtypeStruct(array.shape, array.dtype) for array in staged),
        ],
        [HBM] * (3 + STAGED),
        in_hbm(faces, field, stencil, *staged),
        out_specs=[HBM] + [VMEM] * (5 + STAGED),
        scratch=[
            pltpu.SMEM(faces.shape, jnp.int32),
            pltpu.SMEM(stencil.shape, jnp.float32),
            pltpu.VMEM((2, V, CX, 8, z), jnp.float32),
            pltpu.VMEM((FACES * FACES, SLOT * V, z), jnp.float32),
            pltpu.VMEM(shape, jnp.float32),
            pltpu.SemaphoreType.DMA((6 + STAGED,)),
            pltpu.SemaphoreType.DMA((PIECES,)),
        ],
    )


def patch_kernel(strips_ref, old_inner_ref, old_outer_ref, inner_ref, outer_ref):
    rows = inner_ref.shape[1]
    at = inner_plane()
    for ref, old, plane in (
        (inner_ref, old_inner_ref, at),
        (outer_ref, old_outer_ref, 1 - at),
    ):
        ref[...] = old[...]
        for side, row in enumerate(edge_rows(rows)):
            for var in range(V):
                here = side * V + var
                ref[var, row : row + 1, :] = strips_ref[plane, here : here + 1, :]


def patch_part(strips, inner, outer):
    shape = f32(*inner.shape)
    return call(patch_kernel, [shape, shape], [VMEM] * 3, (strips, inner, outer))


def setup_kernel(
    live_ref, source_ref, target_ref, weight_ref, inverse_ref, matrix_ref, edge_ref
):
    entries = target_ref.shape[1]
    columns = matrix_ref.shape[1]
    groups = columns // (SLOT * V)
    row_ids = lax.broadcasted_iota(jnp.int32, (ROWS, entries), 0)
    entry_ids = lax.broadcasted_iota(jnp.int32, (ROWS, entries), 1)
    chosen = (row_ids // V == target_ref[...]) & (entry_ids < live_ref[0, 0])
    slots = lax.rem(lax.broadcasted_iota(jnp.int32, (1, entries), 1), SLOT)
    place = SLOT * (groups - 1 - source_ref[...]) + slots
    shift = lax.broadcasted_iota(jnp.int32, (columns, entries), 0) - place * V
    matrix = jnp.zeros(matrix_ref.shape, jnp.float32)
    for col in range(V):
        spread = jnp.concatenate(
            [jnp.where(chosen, weight_ref[var, col : col + 1, :], 0.0) for var in range(V)],
            axis=0,
        )
        high = spread.astype(jnp.bfloat16)
        low = (spread - high.astype(jnp.float32)).astype(jnp.bfloat16)
        order = (shift == col).astype(jnp.float32).astype(jnp.bfloat16)
        matrix = matrix + lax.dot_general(
            jnp.concatenate([high, low], axis=0),
            order,
            (((1,), (1,)), ((), ())),
            preferred_element_type=jnp.float32,
        )
    matrix_ref[...] = matrix.astype(jnp.bfloat16)
    for plane in range(CX):
        for side, row in enumerate(edge_rows(inverse_ref.shape[3])):
            for var in range(V):
                to = side * V + var
                for col in range(V):
                    edge_ref[col, plane, to : to + 1, :] = (
                        relax_weight * inverse_ref[var, col, plane, row : row + 1, :]
                    )


def setup_part(live, source, target, weight, inverse, groups):
    return call(
        setup_kernel,
        [
            jax.ShapeDtypeStruct((2 * V * ROWS, groups * SLOT * V), jnp.bfloat16),
            f32(V, CX, 2 * V, inverse.shape[-1]),
        ],
        [SMEM] + [VMEM] * 4,
        (live, source, target, weight, inverse),
    )


def times(coef, value):
    rows, lanes = value.shape
    return (value.reshape(rows // 8, 8, lanes) * coef).reshape(rows, lanes)


def near_kernel(
    coefs_ref, inner_ref, outer_ref, right_ref, conductivity_ref, inner_load_ref, outer_load_ref
):
    rows, lanes = inner_ref.shape[1:]
    row_ids = lax.broadcasted_iota(jnp.int32, (rows, lanes), 0)
    lane_ids = lax.broadcasted_iota(jnp.int32, (rows, lanes), 1)
    at = inner_plane()
    for here, beside, plane, out_ref in (
        (inner_ref, outer_ref, at, inner_load_ref),
        (outer_ref, inner_ref, 1 - at, outer_load_ref),
    ):
        directions = (1 - plane, 2, 3, 4, 5)
        sums = [jnp.zeros((rows, lanes), jnp.float32) for _ in range(V)]
        for col in range(V):
            value = here[col]
            shifted = (
                beside[col],
                jnp.where(row_ids == 0, 0.0, pltpu.roll(value, 1, 0)),
                jnp.where(row_ids == rows - 1, 0.0, pltpu.roll(value, rows - 1, 0)),
                jnp.where(lane_ids == 0, 0.0, pltpu.roll(value, 1, 1)),
                jnp.where(lane_ids == lanes - 1, 0.0, pltpu.roll(value, lanes - 1, 1)),
            )
            for direction, moved in zip(directions, shifted):
                for var in range(V):
                    sums[var] = sums[var] + times(coefs_ref[direction, var, col], moved)
        cond = conductivity_ref[plane]
        for var in range(V):
            out_ref[var] = right_ref[var, plane] + cond * sums[var]


def near_part(coefs, inner, outer, right, cond):
    return call(
        near_kernel,
        [f32(*inner.shape), f32(*inner.shape)],
        [VMEM] * 5,
        (coefs, inner, outer, right, cond),
        flops=3_000_000,
        moved=1024 * 1024,
    )


def finish(plane, coefs_ref, here_ref, load_ref, outside_ref, conductivity_ref, inverse_ref):
    cond = conductivity_ref[plane]
    loads = []
    for var in range(V):
        total = times(coefs_ref[plane, var, 0], outside_ref[0])
        for col in range(1, V):
            total = total + times(coefs_ref[plane, var, col], outside_ref[col])
        loads.append(load_ref[var] + cond * total)
    values = []
    for var in range(V):
        total = inverse_ref[var, 0, plane] * loads[0]
        for col in range(1, V):
            total = total + inverse_ref[var, col, plane] * loads[col]
        values.append((1.0 - relax_weight) * here_ref[var] + relax_weight * total)
    return values


def outer_kernel(
    coefs_ref,
    here_ref,
    load_ref,
    outside_ref,
    conductivity_ref,
    inverse_ref,
    next_ref,
    strips_ref,
):
    plane = 1 - inner_plane()
    values = finish(
        plane, coefs_ref, here_ref, load_ref, outside_ref, conductivity_ref, inverse_ref
    )
    for var, value in enumerate(values):
        next_ref[var] = value
        for side, row in enumerate(edge_rows(value.shape[0])):
            to = side * V + var
            strips_ref[to : to + 1, :] = value[row : row + 1]


def outer_part(coefs, here, load, outside, cond, inverse):
    return call(
        outer_kernel,
        [f32(*here.shape), f32(2 * V, here.shape[-1])],
        [VMEM] * 6,
        (coefs, here, load, outside, cond, inverse),
        flops=1_000_000,
        moved=1024 * 1024,
    )


def inner_kernel(
    coefs_ref,
    here_ref,
    load_ref,
    outside_ref,
    conductivity_ref,
    inverse_ref,
    other_ref,
    next_ref,
    strips_ref,
):
    plane = inner_plane()
    strips_ref[1 - plane] = other_ref[...]
    values = finish(
        plane, coefs_ref, here_ref, load_ref, outside_ref, conductivity_ref, inverse_ref
    )
    for var, value in enumerate(values):
        next_ref[var] = value
        for side, row in enumerate(edge_rows(value.shape[0])):
            to = side * V + var
            strips_ref[plane, to : to + 1, :] = value[row : row + 1]


def inner_part(coefs, here, load, outside, cond, inverse, other):
    return call(
        inner_kernel,
        [f32(*here.shape), f32(CX, *other.shape)],
        [VMEM] * 7,
        (coefs, here, load, outside, cond, inverse, other),
        flops=1_000_000,
        moved=1024 * 1024,
    )


def new_strips(matrix_ref, edge_ref, strips_ref, got_ref):
    groups, block, z = got_ref.shape
    values = got_ref[...].reshape(groups * block, z)
    high = values.astype(jnp.bfloat16)
    low = (values - high.astype(jnp.float32)).astype(jnp.bfloat16)
    count = V * ROWS
    both = jnp.dot(matrix_ref[...], high, preferred_element_type=jnp.float32)
    rest = jnp.dot(matrix_ref[:count, :], low, preferred_element_type=jnp.float32)
    added = both[:count] + (both[count:] + rest)
    tiles = []
    for plane in range(CX):
        total = strips_ref[plane]
        for col in range(V):
            begin = col * ROWS + plane * 2 * V
            total = total + edge_ref[col, plane] * added[begin : begin + 2 * V]
        tiles.append(total)
    return tiles


def strip_kernel(
    matrix_ref, edge_ref, strips_ref, got_ref, mask_ref, send_hbm, new_ref, block, sems
):
    tiles = new_strips(matrix_ref, edge_ref, strips_ref, got_ref)
    for plane, tile in enumerate(tiles):
        new_ref[plane] = tile
    upper, above, below = face_halves(tiles)
    faces = [jnp.where(upper, above[face], below[face]) for face in range(FACES)]

    def fill(group):
        mask = mask_ref[group]
        value = faces[FACES - 1]
        for face in range(FACES - 1):
            value = jnp.where(mask == face, faces[face], value)
        return value

    for copy in send_pieces(block, send_hbm, sems, fill):
        copy.wait()


def strip_part(matrix, edge, strips, got, mask):
    return call(
        strip_kernel,
        [f32(*got.shape), f32(*strips.shape)],
        [VMEM] * 5,
        (matrix, edge, strips, got, mask),
        out_specs=[HBM, VMEM],
        scratch=[pltpu.VMEM(got.shape, jnp.float32), pltpu.SemaphoreType.DMA((PIECES,))],
    )


def last_kernel(
    matrix_ref, edge_ref, strips_ref, got_ref, inner_ref, outer_ref, out_hbm, edges, sems
):
    rows = inner_ref.shape[1]
    tile = edges.shape[3]
    at = inner_plane()
    middle = pl.ds(tile, rows - 2 * tile)
    copies = [
        pltpu.make_async_copy(
            ref.at[:, middle], out_hbm.at[:, plane, middle], sems.at[number]
        )
        for number, (ref, plane) in enumerate(((inner_ref, at), (outer_ref, 1 - at)))
    ]
    for copy in copies:
        copy.start()
    starts = (0, rows - tile)
    for ref, plane in ((inner_ref, at), (outer_ref, 1 - at)):
        for side, start in enumerate(starts):
            for var in range(V):
                edges[side, var, plane] = ref[var, start : start + tile, :]
    tiles = new_strips(matrix_ref, edge_ref, strips_ref, got_ref)
    for plane, value in enumerate(tiles):
        for side, row in enumerate((0, tile - 1)):
            for var in range(V):
                here = side * V + var
                edges[side, var, plane, row : row + 1, :] = value[here : here + 1]
    for side, start in enumerate(starts):
        copies.append(
            pltpu.make_async_copy(
                edges.at[side], out_hbm.at[:, :, pl.ds(start, tile)], sems.at[2 + side]
            )
        )
        copies[-1].start()
    for copy in copies:
        copy.wait()


def last_part(matrix, edge, strips, got, inner, outer):
    rows, z = inner.shape[1:]
    return call(
        last_kernel,
        [f32(V, CX, rows, z)],
        [VMEM] * 6,
        (matrix, edge, strips, got, inner, outer),
        out_specs=[HBM],
        scratch=[pltpu.VMEM((2, V, CX, 8, z), jnp.float32), pltpu.SemaphoreType.DMA((4,))],
    )[0]


def per_device(
    right_side,
    initial,
    block_inverse,
    conductivity,
    stencil,
    coupling_source,
    coupling_target,
    coupling_weight,
    live_count,
    send_faces,
):
    field = initial[0]
    right = right_side[0]
    inverse = block_inverse[0]
    cond = conductivity[0]
    coefs = jnp.transpose(stencil[0], (1, 2, 0))
    weight = jnp.transpose(coupling_weight[0, 0], (1, 2, 0))
    faces = jnp.transpose(send_faces[0, 0], (1, 0))

    count = lax.axis_size("within")
    core_swap = [(i, i ^ 1) for i in range(count)]
    chip_swap = [(i, i + 1) for i in range(1, count - 1, 2)]
    chip_swap += [(j, i) for i, j in chip_swap]

    send, new, inner, outer, mask, coefs, *staged = first_part(
        faces,
        field,
        coefs,
        right,
        cond,
        inverse,
        coupling_source[0],
        coupling_target[0],
        weight,
    )
    right, cond, inverse, source, target, weight = staged
    matrix, edge = setup_part(live_count, source, target, weight, inverse, faces.shape[1])
    members = [list(reversed(range(lax.axis_size("dom"))))]
    for sweep in range(SWEEPS):
        got = lax.all_to_all(send, "dom", 0, 0, tiled=True, axis_index_groups=members)
        inner, outer = patch_part(new, inner, outer)
        from_chip = lax.ppermute(outer, "within", chip_swap)
        from_core = lax.ppermute(inner, "within", core_swap)
        inner_load, outer_load = near_part(coefs, inner, outer, right, cond)
        outer, rows = outer_part(coefs, outer, outer_load, from_chip, cond, inverse)
        inner, strips = inner_part(coefs, inner, inner_load, from_core, cond, inverse, rows)
        if sweep < SWEEPS - 1:
            send, new = strip_part(matrix, edge, strips, got, mask)
        else:
            out = last_part(matrix, edge, strips, got, inner, outer)
    return out[None]


def solution(mesh):
    in_specs = (
        P("dom", None, "within", None, None),
        P("dom", None, "within", None, None),
        P("dom", None, None, "within", None, None),
        P("dom", "within", None, None),
        P("dom", None, None, None),
        P("dom", "within", None),
        P("dom", "within", None),
        P("dom", "within", None, None, None),
        P("dom", "within"),
        P("dom", "within", None, None),
    )
    out_specs = P("dom", None, "within", None, None)
    return jax.shard_map(
        per_device, mesh=mesh, in_specs=in_specs, out_specs=out_specs, check_vma=False
    )
```

```python
import functools

import jax
import jax.numpy as jnp
from jax import lax
from jax.experimental import pallas as pl
from jax.experimental.pallas import tpu as pltpu
from jax.sharding import PartitionSpec as P

SWEEPS = 3
V = 4
CX = 2
FACES = 4
SLOT = 2
ROWS = FACES * V
PIECES = 4
STAGED = 6

relax_weight = 0.8

VMEM = pl.BlockSpec(memory_space=pltpu.VMEM)
SMEM = pl.BlockSpec(memory_space=pltpu.SMEM)
HBM = pl.BlockSpec(memory_space=pltpu.HBM)
PARAMS = pltpu.CompilerParams(vmem_limit_bytes=24 * 1024 * 1024)


def call(
    kernel, out_shape, in_specs, args, out_specs=None, scratch=(), flops=0, moved=512 * 1024
):
    return pl.pallas_call(
        kernel,
        out_shape=out_shape,
        in_specs=in_specs,
        out_specs=out_specs or [VMEM] * len(out_shape),
        scratch_shapes=list(scratch),
        compiler_params=PARAMS,
        cost_estimate=pl.CostEstimate(flops=flops, bytes_accessed=moved, transcendentals=0),
    )(*args)


def in_hbm(*arrays):
    return tuple(pltpu.with_memory_space_constraint(array, pltpu.HBM) for array in arrays)


def f32(*shape):
    return jax.ShapeDtypeStruct(shape, jnp.float32)


def inner_plane():
    return 1 - lax.rem(lax.axis_index("within"), 2)


def edge_rows(rows):
    return (0, rows - 1)


def face_halves(tiles):
    upper = lax.broadcasted_iota(jnp.int32, tiles[0].shape, 0) < V
    above, below = [], []
    for tile in tiles:
        other = pltpu.roll(tile, V, 0)
        above += [tile, other]
        below += [other, tile]
    return upper, above, below


def send_pieces(block, send_hbm, sems, fill):
    pieces = sems.shape[0]
    size = block.shape[0] // pieces
    copies = []
    for piece in range(pieces):
        for place in range(piece * size, (piece + 1) * size):
            block[place] = fill(block.shape[0] - 1 - place)
        part = pl.ds(piece * size, size)
        copies.append(pltpu.make_async_copy(block.at[part], send_hbm.at[part], sems.at[piece]))
        copies[-1].start()
    return copies


def first_kernel(
    live_ref,
    faces_hbm,
    field_hbm,
    stencil_hbm,
    *refs,
):
    staged_hbm, refs = refs[:STAGED], refs[STAGED:]
    send_hbm, strips_ref, inner_ref, outer_ref, mask_ref, coefs_ref = refs[:6]
    matrix_ref, edge_ref = refs[6:8]
    staged, refs = refs[8 : 8 + STAGED], refs[8 + STAGED :]
    faces, stencil, edges, choices, block, sems, send_sems = refs
    rows = field_hbm.shape[2]
    tile = edges.shape[3]
    at = inner_plane()
    pairs = [
        (faces_hbm, faces),
        (field_hbm.at[:, :, pl.ds(0, tile)], edges.at[0]),
        (field_hbm.at[:, :, pl.ds(rows - tile, tile)], edges.at[1]),
        (stencil_hbm, stencil),
        (field_hbm.at[:, at], inner_ref),
        (field_hbm.at[:, 1 - at], outer_ref),
        *zip(staged_hbm, staged),
    ]
    copies = [
        pltpu.make_async_copy(here, there, sems.at[number])
        for number, (here, there) in enumerate(pairs)
    ]
    for copy in copies:
        copy.start()
    for copy in copies[:3]:
        copy.wait()
    for plane in range(CX):
        for side, row in enumerate((0, tile - 1)):
            for var in range(V):
                to = side * V + var
                strips_ref[plane, to : to + 1, :] = edges[side, var, plane, row : row + 1, :]
    upper, above, below = face_halves([strips_ref[plane] for plane in range(CX)])
    for face in range(FACES):
        for other in range(FACES):
            choices[face * FACES + other] = jnp.where(upper, above[face], below[other])

    def fill(group):
        return choices[faces[0, group] * FACES + faces[1, group]]

    sends = send_pieces(block, send_hbm, send_sems, fill)
    for group in range(mask_ref.shape[0]):
        mask_ref[group] = jnp.where(upper, faces[0, group], faces[1, group])
    copies[3].wait()
    for direction in range(6):
        for var in range(V):
            for col in range(V):
                coefs_ref[direction, var, col] = jnp.full(
                    coefs_ref.shape[3:], stencil[var, col, direction], jnp.float32
                )
    for copy in copies[4:]:
        copy.wait()
    _, _, inverse_ref, source_ref, target_ref, weight_ref = staged
    setup(live_ref, source_ref, target_ref, weight_ref, inverse_ref, matrix_ref, edge_ref)
    for copy in sends:
        copy.wait()


def first_part(live, faces, field, stencil, *staged):
    groups, (rows, z) = faces.shape[1], field.shape[2:]
    shape = (groups, SLOT * V, z)
    return call(
        first_kernel,
        [
            f32(*shape),
            f32(CX, 2 * V, z),
            f32(V, rows, z),
            f32(V, rows, z),
            jax.ShapeDtypeStruct(shape, jnp.int32),
            f32(6, V, V, 8, z),
            jax.ShapeDtypeStruct((2 * V * ROWS, groups * SLOT * V), jnp.bfloat16),
            f32(V, CX, 2 * V, z),
            *(jax.ShapeDtypeStruct(array.shape, array.dtype) for array in staged),
        ],
        [SMEM] + [HBM] * (3 + STAGED),
        (live, *in_hbm(faces, field, stencil, *staged)),
        out_specs=[HBM] + [VMEM] * (7 + STAGED),
        scratch=[
            pltpu.SMEM(faces.shape, jnp.int32),
            pltpu.SMEM(stencil.shape, jnp.float32),
            pltpu.VMEM((2, V, CX, 8, z), jnp.float32),
            pltpu.VMEM((FACES * FACES, SLOT * V, z), jnp.float32),
            pltpu.VMEM(shape, jnp.float32),
            pltpu.SemaphoreType.DMA((6 + STAGED,)),
            pltpu.SemaphoreType.DMA((PIECES,)),
        ],
    )


def patch_kernel(strips_ref, old_inner_ref, old_outer_ref, inner_ref, outer_ref):
    rows = inner_ref.shape[1]
    at = inner_plane()
    for ref, old, plane in (
        (inner_ref, old_inner_ref, at),
        (outer_ref, old_outer_ref, 1 - at),
    ):
        ref[...] = old[...]
        for side, row in enumerate(edge_rows(rows)):
            for var in range(V):
                here = side * V + var
                ref[var, row : row + 1, :] = strips_ref[plane, here : here + 1, :]


def patch_part(strips, inner, outer):
    shape = f32(*inner.shape)
    return call(patch_kernel, [shape, shape], [VMEM] * 3, (strips, inner, outer))


def setup(
    live_ref, source_ref, target_ref, weight_ref, inverse_ref, matrix_ref, edge_ref
):
    entries = target_ref.shape[1]
    columns = matrix_ref.shape[1]
    groups = columns // (SLOT * V)
    row_ids = lax.broadcasted_iota(jnp.int32, (ROWS, entries), 0)
    entry_ids = lax.broadcasted_iota(jnp.int32, (ROWS, entries), 1)
    chosen = (row_ids // V == target_ref[...]) & (entry_ids < live_ref[0, 0])
    slots = lax.rem(lax.broadcasted_iota(jnp.int32, (1, entries), 1), SLOT)
    place = SLOT * (groups - 1 - source_ref[...]) + slots
    shift = lax.broadcasted_iota(jnp.int32, (columns, entries), 0) - place * V
    matrix = jnp.zeros(matrix_ref.shape, jnp.float32)
    for col in range(V):
        spread = jnp.concatenate(
            [jnp.where(chosen, weight_ref[var, col : col + 1, :], 0.0) for var in range(V)],
            axis=0,
        )
        high = spread.astype(jnp.bfloat16)
        low = (spread - high.astype(jnp.float32)).astype(jnp.bfloat16)
        order = (shift == col).astype(jnp.float32).astype(jnp.bfloat16)
        matrix = matrix + lax.dot_general(
            jnp.concatenate([high, low], axis=0),
            order,
            (((1,), (1,)), ((), ())),
            preferred_element_type=jnp.float32,
        )
    matrix_ref[...] = matrix.astype(jnp.bfloat16)
    for plane in range(CX):
        for side, row in enumerate(edge_rows(inverse_ref.shape[3])):
            for var in range(V):
                to = side * V + var
                for col in range(V):
                    edge_ref[col, plane, to : to + 1, :] = (
                        relax_weight * inverse_ref[var, col, plane, row : row + 1, :]
                    )


def times(coef, value):
    rows, lanes = value.shape
    return (value.reshape(rows // 8, 8, lanes) * coef).reshape(rows, lanes)


def near_kernel(
    coefs_ref, inner_ref, outer_ref, right_ref, conductivity_ref, inner_load_ref, outer_load_ref
):
    rows, lanes = inner_ref.shape[1:]
    row_ids = lax.broadcasted_iota(jnp.int32, (rows, lanes), 0)
    lane_ids = lax.broadcasted_iota(jnp.int32, (rows, lanes), 1)
    at = inner_plane()
    for here, beside, plane, out_ref in (
        (inner_ref, outer_ref, at, inner_load_ref),
        (outer_ref, inner_ref, 1 - at, outer_load_ref),
    ):
        directions = (1 - plane, 2, 3, 4, 5)
        sums = [jnp.zeros((rows, lanes), jnp.float32) for _ in range(V)]
        for col in range(V):
            value = here[col]
            shifted = (
                beside[col],
                jnp.where(row_ids == 0, 0.0, pltpu.roll(value, 1, 0)),
                jnp.where(row_ids == rows - 1, 0.0, pltpu.roll(value, rows - 1, 0)),
                jnp.where(lane_ids == 0, 0.0, pltpu.roll(value, 1, 1)),
                jnp.where(lane_ids == lanes - 1, 0.0, pltpu.roll(value, lanes - 1, 1)),
            )
            for direction, moved in zip(directions, shifted):
                for var in range(V):
                    sums[var] = sums[var] + times(coefs_ref[direction, var, col], moved)
        cond = conductivity_ref[plane]
        for var in range(V):
            out_ref[var] = right_ref[var, plane] + cond * sums[var]


def near_part(coefs, inner, outer, right, cond):
    return call(
        near_kernel,
        [f32(*inner.shape), f32(*inner.shape)],
        [VMEM] * 5,
        (coefs, inner, outer, right, cond),
        flops=3_000_000,
        moved=1024 * 1024,
    )


def finish(plane, coefs_ref, here_ref, load_ref, outside_ref, conductivity_ref, inverse_ref):
    cond = conductivity_ref[plane]
    loads = []
    for var in range(V):
        total = times(coefs_ref[plane, var, 0], outside_ref[0])
        for col in range(1, V):
            total = total + times(coefs_ref[plane, var, col], outside_ref[col])
        loads.append(load_ref[var] + cond * total)
    values = []
    for var in range(V):
        total = inverse_ref[var, 0, plane] * loads[0]
        for col in range(1, V):
            total = total + inverse_ref[var, col, plane] * loads[col]
        values.append((1.0 - relax_weight) * here_ref[var] + relax_weight * total)
    return values


def outer_kernel(
    coefs_ref,
    here_ref,
    load_ref,
    outside_ref,
    conductivity_ref,
    inverse_ref,
    next_ref,
    strips_ref,
):
    plane = 1 - inner_plane()
    values = finish(
        plane, coefs_ref, here_ref, load_ref, outside_ref, conductivity_ref, inverse_ref
    )
    for var, value in enumerate(values):
        next_ref[var] = value
        for side, row in enumerate(edge_rows(value.shape[0])):
            to = side * V + var
            strips_ref[to : to + 1, :] = value[row : row + 1]


def outer_part(coefs, here, load, outside, cond, inverse):
    return call(
        outer_kernel,
        [f32(*here.shape), f32(2 * V, here.shape[-1])],
        [VMEM] * 6,
        (coefs, here, load, outside, cond, inverse),
        flops=1_000_000,
        moved=1024 * 1024,
    )


def inner_kernel(
    coefs_ref,
    here_ref,
    load_ref,
    outside_ref,
    conductivity_ref,
    inverse_ref,
    other_ref,
    next_ref,
    strips_ref,
):
    plane = inner_plane()
    strips_ref[1 - plane] = other_ref[...]
    values = finish(
        plane, coefs_ref, here_ref, load_ref, outside_ref, conductivity_ref, inverse_ref
    )
    for var, value in enumerate(values):
        next_ref[var] = value
        for side, row in enumerate(edge_rows(value.shape[0])):
            to = side * V + var
            strips_ref[plane, to : to + 1, :] = value[row : row + 1]


def inner_part(coefs, here, load, outside, cond, inverse, other):
    return call(
        inner_kernel,
        [f32(*here.shape), f32(CX, *other.shape)],
        [VMEM] * 7,
        (coefs, here, load, outside, cond, inverse, other),
        flops=1_000_000,
        moved=1024 * 1024,
    )


def new_strips(matrix_ref, edge_ref, strips_ref, got_ref):
    groups, block, z = got_ref.shape
    values = got_ref[...].reshape(groups * block, z)
    high = values.astype(jnp.bfloat16)
    low = (values - high.astype(jnp.float32)).astype(jnp.bfloat16)
    count = V * ROWS
    both = jnp.dot(matrix_ref[...], high, preferred_element_type=jnp.float32)
    rest = jnp.dot(matrix_ref[:count, :], low, preferred_element_type=jnp.float32)
    added = both[:count] + (both[count:] + rest)
    tiles = []
    for plane in range(CX):
        total = strips_ref[plane]
        for col in range(V):
            begin = col * ROWS + plane * 2 * V
            total = total + edge_ref[col, plane] * added[begin : begin + 2 * V]
        tiles.append(total)
    return tiles


def strip_kernel(
    matrix_ref, edge_ref, strips_ref, got_ref, mask_ref, send_hbm, new_ref, block, sems
):
    tiles = new_strips(matrix_ref, edge_ref, strips_ref, got_ref)
    for plane, tile in enumerate(tiles):
        new_ref[plane] = tile
    upper, above, below = face_halves(tiles)
    faces = [jnp.where(upper, above[face], below[face]) for face in range(FACES)]

    def fill(group):
        mask = mask_ref[group]
        value = faces[FACES - 1]
        for face in range(FACES - 1):
            value = jnp.where(mask == face, faces[face], value)
        return value

    for copy in send_pieces(block, send_hbm, sems, fill):
        copy.wait()


def strip_part(matrix, edge, strips, got, mask):
    return call(
        strip_kernel,
        [f32(*got.shape), f32(*strips.shape)],
        [VMEM] * 5,
        (matrix, edge, strips, got, mask),
        out_specs=[HBM, VMEM],
        scratch=[pltpu.VMEM(got.shape, jnp.float32), pltpu.SemaphoreType.DMA((PIECES,))],
    )


def last_kernel(
    matrix_ref, edge_ref, strips_ref, got_ref, inner_ref, outer_ref, out_hbm, edges, sems
):
    rows = inner_ref.shape[1]
    tile = edges.shape[3]
    at = inner_plane()
    middle = pl.ds(tile, rows - 2 * tile)
    copies = [
        pltpu.make_async_copy(
            ref.at[:, middle], out_hbm.at[:, plane, middle], sems.at[number]
        )
        for number, (ref, plane) in enumerate(((inner_ref, at), (outer_ref, 1 - at)))
    ]
    for copy in copies:
        copy.start()
    starts = (0, rows - tile)
    for ref, plane in ((inner_ref, at), (outer_ref, 1 - at)):
        for side, start in enumerate(starts):
            for var in range(V):
                edges[side, var, plane] = ref[var, start : start + tile, :]
    tiles = new_strips(matrix_ref, edge_ref, strips_ref, got_ref)
    for plane, value in enumerate(tiles):
        for side, row in enumerate((0, tile - 1)):
            for var in range(V):
                here = side * V + var
                edges[side, var, plane, row : row + 1, :] = value[here : here + 1]
    for side, start in enumerate(starts):
        copies.append(
            pltpu.make_async_copy(
                edges.at[side], out_hbm.at[:, :, pl.ds(start, tile)], sems.at[2 + side]
            )
        )
        copies[-1].start()
    for copy in copies:
        copy.wait()


def last_part(matrix, edge, strips, got, inner, outer):
    rows, z = inner.shape[1:]
    return call(
        last_kernel,
        [f32(V, CX, rows, z)],
        [VMEM] * 6,
        (matrix, edge, strips, got, inner, outer),
        out_specs=[HBM],
        scratch=[pltpu.VMEM((2, V, CX, 8, z), jnp.float32), pltpu.SemaphoreType.DMA((4,))],
    )[0]


def per_device(
    right_side,
    initial,
    block_inverse,
    conductivity,
    stencil,
    coupling_source,
    coupling_target,
    coupling_weight,
    live_count,
    send_faces,
):
    field = initial[0]
    right = right_side[0]
    inverse = block_inverse[0]
    cond = conductivity[0]
    coefs = jnp.transpose(stencil[0], (1, 2, 0))
    weight = jnp.transpose(coupling_weight[0, 0], (1, 2, 0))
    faces = jnp.transpose(send_faces[0, 0], (1, 0))

    count = lax.axis_size("within")
    core_swap = [(i, i ^ 1) for i in range(count)]
    chip_swap = [(i, i + 1) for i in range(1, count - 1, 2)]
    chip_swap += [(j, i) for i, j in chip_swap]

    send, new, inner, outer, mask, coefs, matrix, edge, *staged = first_part(
        live_count,
        faces,
        field,
        coefs,
        right,
        cond,
        inverse,
        coupling_source[0],
        coupling_target[0],
        weight,
    )
    right, cond, inverse = staged[:3]
    members = [list(reversed(range(lax.axis_size("dom"))))]
    for sweep in range(SWEEPS):
        got = lax.all_to_all(send, "dom", 0, 0, tiled=True, axis_index_groups=members)
        inner, outer = patch_part(new, inner, outer)
        from_chip = lax.ppermute(outer, "within", chip_swap)
        from_core = lax.ppermute(inner, "within", core_swap)
        inner_load, outer_load = near_part(coefs, inner, outer, right, cond)
        outer, rows = outer_part(coefs, outer, outer_load, from_chip, cond, inverse)
        inner, strips = inner_part(coefs, inner, inner_load, from_core, cond, inverse, rows)
        if sweep < SWEEPS - 1:
            send, new = strip_part(matrix, edge, strips, got, mask)
        else:
            out = last_part(matrix, edge, strips, got, inner, outer)
    return out[None]


def solution(mesh):
    in_specs = (
        P("dom", None, "within", None, None),
        P("dom", None, "within", None, None),
        P("dom", None, None, "within", None, None),
        P("dom", "within", None, None),
        P("dom", None, None, None),
        P("dom", "within", None),
        P("dom", "within", None),
        P("dom", "within", None, None, None),
        P("dom", "within"),
        P("dom", "within", None, None),
    )
    out_specs = P("dom", None, "within", None, None)
    return jax.shard_map(
        per_device, mesh=mesh, in_specs=in_specs, out_specs=out_specs, check_vma=False
    )
```
